128 devices in a mesh: dp: 8 (over x, z_hi), stream: 16 (over y, z_lo, core).
Axes of the slice: x: 4, y: 4, z: 4 (z_hi: 2, z_lo: 2; z = z_hi * 2 + z_lo), core: 2. Of those that a mesh axis runs over, the one named last changes fastest.
Arguments:
- source_embed: bfloat16 [32768, 256], P(('dp', 'stream')), may hold values from -6 to 6
- source_labels: int32 [32768], P(('dp', 'stream')), may hold values from 0 to 63
- target_embed: bfloat16 [8192, 256], P('stream'), may hold values from -6 to 6
- target_labels: int32 [8192], P('stream'), may hold values from 0 to 63
- label_table: bfloat16 [64, 64], replicated, may hold values from 0 to 2
Outputs:
- source_potential: float32 [32768], P(('dp', 'stream'))
- target_dual: float32 [8192], P('stream')
The draws below stay inside these ranges and needn't reach their ends.
All inputs are finite; a program needn't handle non-finite values.
Results may differ from the reference program's by a relative error of at most 0.0003.
Values may be sent and summed in bfloat16 or wider, within the bound.
A program may use at most 64 MiB of HBM per device.

```python
import math
import jax
import jax.numpy as jnp
from jax import lax

E = 256
LABELS = 64
SRC_DEV = 256
TGT_DEV = 512
ITERS = 3
SOURCE_COUNT = 32768
TARGET_COUNT = 8192
N_STREAM = 16


def touch_ends(result, key, low, largest):
    shape = result.shape
    place = [jax.random.randint(jax.random.fold_in(key, axis), (), 0, shape[axis]) for axis in range(len(shape))]
    result = result.at[tuple(place)].set(low)
    longest = shape.index(max(shape))
    place[longest] = (place[longest] + 1) % shape[longest]
    return result.at[tuple(place)].set(largest)


def levels(own_key, shape, split, least, largest):
    gain = 1.0
    for dim, blocks in split:
        draws = jax.random.uniform(jax.random.fold_in(jax.random.fold_in(own_key, 6), dim), (blocks,), jnp.float32, least / len(split), largest / len(split))
        gain = gain * jnp.repeat(jnp.exp(draws), shape[dim] // blocks).reshape((-1,) + (1,) * (len(shape) - 1 - dim))
    return gain


def bell_draw(rng, dims, deviation, bound, shards=(), kind=jnp.bfloat16):
    gain = levels(rng, dims, shards, -0.22, 0.18) if shards else 1.0
    array = jax.random.normal(rng, dims, jnp.float32) * deviation * gain
    return jnp.minimum(jnp.maximum(array, -bound), bound).astype(kind)


def setup_inputs(seed: int = 0) -> dict:
    splits = jax.random.split(jax.random.key(seed), 6)
    source_embed = bell_draw(splits[0], (SOURCE_COUNT, E), 1.0, 6.0, ((0, 128),))
    source_labels = touch_ends(jax.random.randint(splits[1], (SOURCE_COUNT,), 0, LABELS), jax.random.fold_in(splits[1], 1), 0, LABELS - 1).astype(jnp.int32)
    target_embed = bell_draw(splits[2], (TARGET_COUNT, E), 1.0, 6.0, ((0, 16),))
    target_labels = touch_ends(jax.random.randint(splits[3], (TARGET_COUNT,), 0, LABELS), jax.random.fold_in(splits[3], 1), 0, LABELS - 1).astype(jnp.int32)
    label_table = jnp.clip(jax.random.uniform(splits[4], (LABELS, LABELS), jnp.float32, 0.0, 2.0), 0.0, 2.0).astype(jnp.bfloat16)
    return dict(source_embed=source_embed, source_labels=source_labels, target_embed=target_embed, target_labels=target_labels, label_table=label_table)


entropic_scale = 0.02


def pair_costs(xb, lb, yb, mb, table):
    xn = jnp.sum(jnp.square(xb.astype(jnp.float32)), axis=1) / E
    yn = jnp.sum(jnp.square(yb.astype(jnp.float32)), axis=1) / E
    cross = jnp.dot(xb, yb.T, preferred_element_type=jnp.float32)
    labelled = table.astype(jnp.float32)[lb][:, mb]
    return xn[:, None] + yn[None, :] - (2.0 / E) * cross + labelled


def reference(source_embed, source_labels, target_embed, target_labels, label_table):
    group = SRC_DEV * N_STREAM
    src_blocks = source_embed.reshape(SOURCE_COUNT // group, group, E)
    src_marks = source_labels.reshape(SOURCE_COUNT // group, group)
    tgt_blocks = target_embed.reshape(N_STREAM, TGT_DEV, E)
    tgt_marks = target_labels.reshape(N_STREAM, TGT_DEV)
    target_dual = jnp.zeros((TARGET_COUNT,), jnp.float32)
    source_potential = jnp.zeros((SOURCE_COUNT,), jnp.float32)
    for turn in range(ITERS):
        def row_pass(block, dual_pair=target_dual):
            transport_cost = pair_costs(block[0], block[1], target_embed, target_labels, label_table)
            return -entropic_scale * (jax.nn.logsumexp((dual_pair[None, :] - transport_cost) / entropic_scale, axis=1) - math.log(TARGET_COUNT))

        source_potential = lax.map(row_pass, (src_blocks, src_marks)).reshape(SOURCE_COUNT)

        def col_pass(block, dual_pair=source_potential):
            transport_cost = pair_costs(source_embed, source_labels, block[0], block[1], label_table)
            return -entropic_scale * (jax.nn.logsumexp((dual_pair[:, None] - transport_cost) / entropic_scale, axis=0) - math.log(SOURCE_COUNT))

        target_dual = lax.map(col_pass, (tgt_blocks, tgt_marks)).reshape(TARGET_COUNT)
    return source_potential, target_dual
```

```python
import functools
import math

import jax
import jax.numpy as jnp
from jax import lax
from jax.experimental import pallas as pl
from jax.experimental.pallas import tpu as pltpu
from jax.sharding import PartitionSpec as P

MESH = pl.DeviceIdType.MESH
SCALE = 0.02
LOG2E = 1.0 / math.log(2.0)
COST_TO_BITS = LOG2E / SCALE

SRC = 256
TGT = 512
EMB = 256
LABELS = 64
AUX = 16
CHUNKS = 8
QUARTERS = 4
ROWS = QUARTERS * 256
COLS = CHUNKS * SRC
LANES = 128
TILES = COLS // LANES
NT = (((1,), (1,)), ((), ()))


def place():
    dp, stream = lax.axis_index("dp"), lax.axis_index("stream")
    return dp // 2, stream // 4, (dp % 2) * 2 + (stream // 2) % 2, stream % 2


def device(x, y, z, core):
    x, y, z, core = x % 4, y % 4, z % 4, core % 2
    return (x * 2 + z // 2, y * 4 + (z % 2) * 2 + core)


def split3(value):
    high = value.astype(jnp.bfloat16).astype(jnp.float32)
    rest = value - high
    middle = rest.astype(jnp.bfloat16).astype(jnp.float32)
    return high, middle, rest - middle


def aux_rows(embed, labels):
    wide = embed.astype(jnp.float32)
    square = wide * wide
    high = square.astype(jnp.bfloat16)
    low = (square - high.astype(jnp.float32)).astype(jnp.bfloat16)
    ones = jnp.ones((AUX, EMB), jnp.bfloat16)
    norm = lax.dot_general(ones, high, NT, preferred_element_type=jnp.float32)
    norm += lax.dot_general(ones, low, NT, preferred_element_type=jnp.float32)
    first, second, third = split3(norm * (-128.0 / EMB))
    row = lax.broadcasted_iota(jnp.int32, (AUX, SRC), 0)
    marks = jnp.broadcast_to(labels.astype(jnp.float32), (AUX, SRC))
    out = jnp.where(row == 0, marks, 0.0)
    out = jnp.where(row == 1, first, out)
    out = jnp.where(row == 2, second, out)
    out = jnp.where(row == 3, third, out)
    return out.astype(jnp.bfloat16)


def kernel(
    src_ref, src_labels, tgt_ref, tgt_labels, table, f_out, g_out,
    src, tgt, src_side, tgt_side, block, peak, col_max, weight, weight_now, partial,
    spread, s_msg, t_msg, f_first, g_first,
    in_sem, gather_send, gather_recv, s_send, s_recv, t_send, t_recv,
):
    x, y, z, core = place()
    z_lo = z % 2
    mine = y * 2 + core
    s_peers = [(dy, dc) for dy in range(4) for dc in range(2) if (dy, dc) != (0, 0)]
    t_peers = [(dx, dz) for dx in range(4) for dz in range(4) if (dx, dz) != (0, 0)]
    f32 = jnp.float32

    barrier = pltpu.get_barrier_semaphore()
    for dy, dc in s_peers:
        pl.semaphore_signal(barrier, inc=1, device_id=device(x, y + dy, z, core + dc), device_id_type=MESH)
    for dx, dz in t_peers:
        pl.semaphore_signal(barrier, inc=1, device_id=device(x + dx, y, z + dz, core), device_id_type=MESH)

    loads = [
        pltpu.make_async_copy(src_ref, src.at[mine, pl.ds(0, SRC)], in_sem.at[0]),
        pltpu.make_async_copy(tgt_ref.at[pl.ds(0, 256)], tgt.at[2 * z_lo, pl.ds(0, 256)], in_sem.at[1]),
        pltpu.make_async_copy(tgt_ref.at[pl.ds(256, 256)], tgt.at[2 * z_lo + 1, pl.ds(0, 256)], in_sem.at[2]),
    ]
    for load in loads:
        load.start()
    for load in loads:
        load.wait()
    src[mine, pl.ds(SRC, AUX)] = aux_rows(src[mine, pl.ds(0, SRC)], src_labels[...])
    for half in range(2):
        tgt[2 * z_lo + half, pl.ds(256, AUX)] = aux_rows(
            tgt[2 * z_lo + half, pl.ds(0, 256)], tgt_labels[:, half * 256 : half * 256 + 256]
        )

    pl.semaphore_wait(barrier, len(s_peers) + len(t_peers))

    def send(ref_from, ref_to, k, target):
        copy = pltpu.make_async_remote_copy(
            src_ref=ref_from, dst_ref=ref_to, send_sem=gather_send.at[k], recv_sem=gather_recv.at[k],
            device_id=target, device_id_type=MESH,
        )
        copy.start()
        return copy

    started = [send(src.at[mine], src.at[mine], 0, device(x, y, z, core + 1))]
    started += [send(tgt.at[2 * z_lo + h], tgt.at[2 * z_lo + h], 7 + h, device(x, y, z + 1 - 2 * h, core)) for h in range(2)]
    started += [send(src.at[mine], src.at[mine], k, device(x, y + k, z, core)) for k in (1, 3, 2)]

    def arrived(ref, k):
        pltpu.make_async_copy(ref, ref, gather_recv.at[k]).wait()

    def prepare_source(chunk):
        aux = src[chunk, pl.ds(SRC, AUX)].astype(f32)
        row = lax.broadcasted_iota(jnp.int32, (LANES, SRC), 0)
        side = jnp.where(row.astype(f32) == aux[0:1], 1.0, 0.0)
        side = jnp.where((row >= 67) & (row < 70), 1.0, side)
        for k in range(3):
            side = jnp.where(row == LABELS + k, aux[1 + k : 2 + k], side)
        src_side[chunk] = side.astype(jnp.bfloat16)

    def prepare_target(quarter):
        aux = tgt[quarter, pl.ds(256, AUX)].astype(f32)
        row = lax.broadcasted_iota(jnp.int32, (LABELS, 256), 0)
        onehot = jnp.where(row.astype(f32) == aux[0:1], 1.0, 0.0).astype(jnp.bfloat16)
        costs = jnp.dot(table[...], onehot, preferred_element_type=f32) * -128.0
        rest = jnp.where(row < 3, 1.0, 0.0)
        for k in range(3):
            rest = jnp.where(row == 3 + k, aux[1 + k : 2 + k], rest)
        tgt_side[quarter] = jnp.concatenate([costs, rest], axis=0).T.astype(jnp.bfloat16)

    def cols_of(chunk):
        return pl.ds(pl.multiple_of(chunk * SRC, SRC), SRC)

    def costs(quarter, chunk):
        dot = lax.dot_general(tgt[quarter, pl.ds(0, 256)], src[chunk, pl.ds(0, SRC)], NT, preferred_element_type=f32)
        dot += jnp.dot(tgt_side[quarter], src_side[chunk], preferred_element_type=f32)
        dot = dot * (COST_TO_BITS / 128.0)
        block[pl.ds(pl.multiple_of(quarter * 256, 256), 256), cols_of(chunk)] = dot
        peak[quarter, :, cols_of(chunk)] = jnp.max(dot.reshape(32, 8, SRC), axis=0)

    def first_rows(chunk):
        top = jnp.max(jnp.max(peak[:, :, cols_of(chunk)], axis=0), axis=0, keepdims=True)

        def add(step, total):
            rows = pl.ds(pl.multiple_of(step * 32, 32), 32)
            return total + jnp.exp2(block[rows, cols_of(chunk)] - top)

        total = lax.fori_loop(0, ROWS // 32, add, jnp.zeros((32, SRC), f32), unroll=4)
        s_msg[0, 0, pl.ds(chunk, 1)] = top + jnp.log2(jnp.sum(total, axis=0, keepdims=True))

    own, other = mine, y * 2 + (1 - core)
    prepare_source(own)
    for half in range(2):
        prepare_target(2 * z_lo + half)
        costs(2 * z_lo + half, own)
    arrived(src.at[other], 0)
    prepare_source(other)
    for half in range(2):
        costs(2 * z_lo + half, other)
    away = 2 * (1 - z_lo)
    for half in range(2):
        arrived(tgt.at[away + half], 7 + half)
        prepare_target(away + half)
        costs(away + half, own)
        costs(away + half, other)
    first_rows(own)
    first_rows(other)

    def whole_chunk(chunk):
        prepare_source(chunk)
        for quarter in range(QUARTERS):
            costs(quarter, chunk)
        first_rows(chunk)

    def chunk_at(k, c):
        return ((y - k) % 4) * 2 + c

    def take(k):
        chunk = chunk_at(k, core)
        arrived(src.at[chunk], k)
        started.append(send(src.at[chunk], src.at[chunk], 3 + k, device(x, y, z, core + 1)))

    take(1)
    take(3)
    whole_chunk(chunk_at(1, core))
    whole_chunk(chunk_at(3, core))
    for k in (1, 3):
        arrived(src.at[chunk_at(k, 1 - core)], 3 + k)
        whole_chunk(chunk_at(k, 1 - core))
    take(2)
    whole_chunk(chunk_at(2, core))
    arrived(src.at[chunk_at(2, 1 - core)], 5)
    whole_chunk(chunk_at(2, 1 - core))

    def exchange_s(turn):
        for dy, dc in s_peers:
            pltpu.make_async_remote_copy(
                src_ref=s_msg.at[turn, 0], dst_ref=s_msg.at[turn, dy * 2 + dc],
                send_sem=s_send.at[turn], recv_sem=s_recv.at[turn],
                device_id=device(x, y + dy, z, core + dc), device_id_type=MESH,
            ).start()
        others = s_msg.at[turn, pl.ds(1, 7)]
        pltpu.make_async_copy(others, others, s_recv.at[turn]).wait()

    def exchange_t(turn):
        for dx, dz in t_peers:
            pltpu.make_async_remote_copy(
                src_ref=t_msg.at[turn, 0], dst_ref=t_msg.at[turn, dx * 4 + dz],
                send_sem=t_send.at[turn], recv_sem=t_recv.at[turn],
                device_id=device(x + dx, y, z + dz, core), device_id_type=MESH,
            ).start()
        others = t_msg.at[turn, pl.ds(1, 15)]
        pltpu.make_async_copy(others, others, t_recv.at[turn]).wait()

    def joined(parts):
        top = jnp.max(parts, axis=0)
        return top + jnp.log2(jnp.sum(jnp.exp2(parts - top), axis=0))

    def spread_rows(values):
        for chunk in range(CHUNKS):
            spread[:, chunk * SRC : (chunk + 1) * SRC] = jnp.broadcast_to(values[chunk : chunk + 1], (8, SRC))

    def tile(l):
        return slice(l * LANES, (l + 1) * LANES)

    def as_columns(values, b):
        return jnp.broadcast_to(values[b : b + 1], (LANES, LANES)).T

    exchange_s(0)
    source_count = COLS * 16.0
    target_count = ROWS * 8.0
    f_now = math.log2(target_count) - joined(s_msg[0])
    f_first[...] = f_now
    spread_rows(f_now)

    def first_columns(step, _):
        tops = []
        for s in range(4):
            rows = pl.ds(pl.multiple_of(step * 32 + s * 8, 8), 8)
            top = block[rows, tile(0)] + spread[:, tile(0)]
            for l in range(1, TILES):
                top = jnp.maximum(top, block[rows, tile(l)] + spread[:, tile(l)])
            tops.append(jnp.max(top, axis=1, keepdims=True))
        for s in range(4):
            rows = pl.ds(pl.multiple_of(step * 32 + s * 8, 8), 8)
            top = jnp.broadcast_to(tops[s], (8, LANES))
            total = jnp.zeros((8, LANES), f32)
            for l in range(TILES):
                value = jnp.exp2(block[rows, tile(l)] + (spread[:, tile(l)] - top))
                block[rows, tile(l)] = value
                total = total + value
            col_max[rows, :] = top
            partial[rows, :] = top + jnp.log2(jnp.sum(total, axis=1, keepdims=True))
        return 0

    lax.fori_loop(0, ROWS // 32, first_columns, 0)
    for b in range(8):
        t_msg[0, 0, b : b + 1] = partial[b * LANES : (b + 1) * LANES, :].T[0:1]
    exchange_t(0)
    g_now = math.log2(source_count) - joined(t_msg[0])
    g_first[...] = g_now
    for b in range(8):
        rows = slice(b * LANES, (b + 1) * LANES)
        weight[rows, :] = jnp.exp2(col_max[rows, :] + as_columns(g_now, b))

    def row_sums(weights, turn):
        def add(step, totals):
            for s in range(4):
                rows = pl.ds(pl.multiple_of(step * 32 + s * 8, 8), 8)
                w = weights[rows, :]
                totals = tuple(totals[l] + block[rows, tile(l)] * w for l in range(TILES))
            return totals

        totals = lax.fori_loop(0, ROWS // 32, add, tuple(jnp.zeros((8, LANES), f32) for _ in range(TILES)))
        for l in range(TILES):
            s_msg[turn, 0, l // 2 : l // 2 + 1, tile(l % 2)] = jnp.sum(totals[l], axis=0, keepdims=True)

    def column_sums(turn):
        def add(step, _):
            for s in range(4):
                rows = pl.ds(pl.multiple_of(step * 32 + s * 8, 8), 8)
                total = block[rows, tile(0)] * spread[:, tile(0)]
                for l in range(1, TILES):
                    total = total + block[rows, tile(l)] * spread[:, tile(l)]
                partial[rows, :] = total * weight[rows, :]
            return 0

        lax.fori_loop(0, ROWS // 32, add, 0)
        for b in range(8):
            t_msg[turn, 0, b : b + 1] = jnp.sum(partial[b * LANES : (b + 1) * LANES, :].T, axis=0, keepdims=True)

    for turn in (1, 2):
        row_sums(weight if turn == 1 else weight_now, turn)
        exchange_s(turn)
        u_now = target_count / jnp.sum(s_msg[turn], axis=0)
        spread_rows(u_now)
        column_sums(turn)
        exchange_t(turn)
        v_now = source_count / jnp.sum(t_msg[turn], axis=0)
        if turn == 1:
            for b in range(8):
                rows = slice(b * LANES, (b + 1) * LANES)
                weight_now[rows, :] = weight[rows, :] * as_columns(v_now, b)

    f_first[...] = (f_first[...] + jnp.log2(u_now)) * (1.0 / COST_TO_BITS)
    f_out[...] = f_first[pl.ds(mine, 1)]
    g_first[...] = (g_first[...] + jnp.log2(v_now)) * (1.0 / COST_TO_BITS)
    g_out[...] = g_first[pl.ds(z_lo * 4, 4)]

    for copy in started:
        copy.wait_send()
    for turn in range(3):
        others = s_msg.at[turn, pl.ds(1, 7)]
        pltpu.make_async_copy(others, others, s_send.at[turn]).wait()
        others = t_msg.at[turn, pl.ds(1, 15)]
        pltpu.make_async_copy(others, others, t_send.at[turn]).wait()


def body(source_embed, source_labels, target_embed, target_labels, label_table):
    vmem, hbm = pl.BlockSpec(memory_space=pltpu.VMEM), pl.BlockSpec(memory_space=pl.ANY)
    f32, bf16, dma = jnp.float32, jnp.bfloat16, pltpu.SemaphoreType.DMA
    f, g = pl.pallas_call(
        kernel,
        out_shape=(jax.ShapeDtypeStruct((1, SRC), f32), jax.ShapeDtypeStruct((4, LANES), f32)),
        in_specs=[hbm, vmem, hbm, vmem, vmem],
        out_specs=(vmem, vmem),
        scratch_shapes=[
            pltpu.VMEM((CHUNKS, SRC + AUX, EMB), bf16),
            pltpu.VMEM((QUARTERS, 256 + AUX, EMB), bf16),
            pltpu.VMEM((CHUNKS, LANES, SRC), bf16),
            pltpu.VMEM((QUARTERS, 256, LANES), bf16),
            pltpu.VMEM((ROWS, COLS), f32),
            pltpu.VMEM((QUARTERS, 8, COLS), f32),
            pltpu.VMEM((ROWS, LANES), f32),
            pltpu.VMEM((ROWS, LANES), f32),
            pltpu.VMEM((ROWS, LANES), f32),
            pltpu.VMEM((ROWS, LANES), f32),
            pltpu.VMEM((8, COLS), f32),
            pltpu.VMEM((3, 8, CHUNKS, SRC), f32),
            pltpu.VMEM((3, 16, 8, LANES), f32),
            pltpu.VMEM((CHUNKS, SRC), f32),
            pltpu.VMEM((8, LANES), f32),
            dma((3,)),
            dma((9,)),
            dma((9,)),
            dma((3,)),
            dma((3,)),
            dma((3,)),
            dma((3,)),
        ],
        compiler_params=pltpu.CompilerParams(collective_id=0, has_side_effects=True, vmem_limit_bytes=40 << 20),
    )(
        source_embed,
        source_labels.reshape(1, SRC),
        target_embed,
        target_labels.reshape(1, TGT),
        label_table,
    )
    return f.reshape(SRC), g.reshape(TGT)


def solution(mesh):
    placed = (P(("dp", "stream"), None), P(("dp", "stream")), P("stream", None), P("stream"), P())
    return jax.shard_map(
        body,
        mesh=mesh,
        in_specs=placed,
        out_specs=(P(("dp", "stream")), P("stream")),
        check_vma=False,
    )
```

```python
import functools
import math

import jax
import jax.numpy as jnp
from jax import lax
from jax.experimental import pallas as pl
from jax.experimental.pallas import tpu as pltpu
from jax.sharding import PartitionSpec as P

MESH = pl.DeviceIdType.MESH
SCALE = 0.02
LOG2E = 1.0 / math.log(2.0)
COST_TO_BITS = LOG2E / SCALE

SRC = 256
HALF = 128
TGT = 512
EMB = 256
LABELS = 64
AUX = 16
CHUNKS = 4
QUARTERS = 4
ROWS = QUARTERS * 256
COLS = 2 * CHUNKS * 256
LANES = 128
TILES = COLS // LANES
NT = (((1,), (1,)), ((), ()))


def place():
    dp, stream = lax.axis_index("dp"), lax.axis_index("stream")
    return dp // 2, stream // 4, (dp % 2) * 2 + (stream // 2) % 2, stream % 2


def device(x, y, z, core):
    x, y, z, core = x % 4, y % 4, z % 4, core % 2
    return (x * 2 + z // 2, y * 4 + (z % 2) * 2 + core)


def split3(value):
    high = value.astype(jnp.bfloat16).astype(jnp.float32)
    rest = value - high
    middle = rest.astype(jnp.bfloat16).astype(jnp.float32)
    return high, middle, rest - middle


def aux_rows(embed, labels):
    count = embed.shape[0]
    wide = embed.astype(jnp.float32)
    square = wide * wide
    high = square.astype(jnp.bfloat16)
    low = (square - high.astype(jnp.float32)).astype(jnp.bfloat16)
    ones = jnp.ones((AUX, EMB), jnp.bfloat16)
    norm = lax.dot_general(ones, high, NT, preferred_element_type=jnp.float32)
    norm += lax.dot_general(ones, low, NT, preferred_element_type=jnp.float32)
    first, second, third = split3(norm * (-128.0 / EMB))
    row = lax.broadcasted_iota(jnp.int32, (AUX, count), 0)
    marks = jnp.broadcast_to(labels.astype(jnp.float32), (AUX, count))
    out = jnp.where(row == 0, marks, 0.0)
    out = jnp.where(row == 1, first, out)
    out = jnp.where(row == 2, second, out)
    out = jnp.where(row == 3, third, out)
    return out.astype(jnp.bfloat16)


def kernel(
    src_ref, src_labels, tgt_ref, tgt_labels, table, f_out, g_out,
    src, tgt, src_side, tgt_side, block, plan, peak, col_max, weight, partial,
    spread, s_msg, t_msg, f_first, top_dense, g_first,
    in_sem, gather_send, gather_recv, s_send, s_recv, t_send, t_recv, plane_sem,
):
    x, y, z, core = place()
    z_lo = z % 2
    s_peers = [(dy, dc) for dy in (2, 1, 3, 0) for dc in range(2) if (dy, dc) != (0, 0)]
    t_peers = [(dx, dz) for dx in (2, 1, 3, 0) for dz in (2, 1, 3, 0) if (dx, dz) != (0, 0)]
    f32 = jnp.float32

    near = [device(x, y + k, z, core) for k in (1, 2, 3)] + [device(x, y, z, core + 1)]
    near += [device(x, y, z + k, core) for k in (1, 2, 3)] + [device(x + k, y, z, core) for k in (1, 2, 3)]
    barrier = pltpu.get_barrier_semaphore()
    for target in near:
        pl.semaphore_signal(barrier, inc=1, device_id=target, device_id_type=MESH)

    loads = [
        pltpu.make_async_copy(
            src_ref.at[pl.ds(h * HALF, HALF)], src.at[h, y, core, pl.ds(0, HALF)], in_sem.at[h]
        )
        for h in range(2)
    ]
    loads += [
        pltpu.make_async_copy(
            tgt_ref.at[pl.ds(h * 256, 256)], tgt.at[2 * z_lo + h, pl.ds(0, 256)], in_sem.at[2 + h]
        )
        for h in range(2)
    ]
    for load in loads:
        load.start()
    for h in range(2):
        loads[h].wait()
        src[h, y, core, pl.ds(HALF, AUX), 0:HALF] = aux_rows(
            src[h, y, core, pl.ds(0, HALF)], src_labels[:, h * HALF : (h + 1) * HALF]
        )
    for h in range(2):
        loads[2 + h].wait()
        tgt[2 * z_lo + h, pl.ds(256, AUX)] = aux_rows(
            tgt[2 * z_lo + h, pl.ds(0, 256)], tgt_labels[:, h * 256 : (h + 1) * 256]
        )

    pl.semaphore_wait(barrier, len(near))

    def send(ref, k, target):
        copy = pltpu.make_async_remote_copy(
            src_ref=ref, dst_ref=ref, send_sem=gather_send.at[k], recv_sem=gather_recv.at[k],
            device_id=target, device_id_type=MESH,
        )
        copy.start()
        return copy

    def arrived(ref, k):
        pltpu.make_async_copy(ref, ref, gather_recv.at[k]).wait()

    started = []
    for h in range(2):
        own = src.at[h, y, core]
        started += [send(own, 7 * h + k, device(x, y + k, z, core)) for k in (2, 1, 3)]
        started.append(send(own, 7 * h, device(x, y, z, core + 1)))
        if h == 0:
            started += [
                send(tgt.at[2 * z_lo + q], 14 + q, device(x, y, z + 1 - 2 * q, core)) for q in range(2)
            ]
    for k in (1, 2, 3):
        pl.semaphore_signal(plane_sem, inc=1, device_id=device(x + k, y, z, core), device_id_type=MESH)

    def cols_of(h, chunk):
        return pl.ds(pl.multiple_of((h * CHUNKS + chunk) * 256, 256), 256)

    def prepare_source(h, chunk, slot):
        aux = [src[h, chunk, c, pl.ds(HALF, AUX), 0:HALF].astype(f32) for c in range(2)]
        aux = jnp.concatenate(aux, axis=1)
        row = lax.broadcasted_iota(jnp.int32, (LANES, 256), 0)
        side = jnp.where(row.astype(f32) == aux[0:1], 1.0, 0.0)
        side = jnp.where((row >= 67) & (row < 70), 1.0, side)
        for k in range(3):
            side = jnp.where(row == LABELS + k, aux[1 + k : 2 + k], side)
        src_side[slot] = side.astype(jnp.bfloat16)

    def prepare_target(quarter):
        aux = tgt[quarter, pl.ds(256, AUX)].astype(f32)
        row = lax.broadcasted_iota(jnp.int32, (LABELS, 256), 0)
        onehot = jnp.where(row.astype(f32) == aux[0:1], 1.0, 0.0).astype(jnp.bfloat16)
        costs = jnp.dot(table[...], onehot, preferred_element_type=f32) * -128.0
        rest = jnp.where(row < 3, 1.0, 0.0)
        for k in range(3):
            rest = jnp.where(row == 3 + k, aux[1 + k : 2 + k], rest)
        tgt_side[quarter] = jnp.concatenate([costs, rest], axis=0).T.astype(jnp.bfloat16)

    def costs(quarter, h, chunk, slot):
        rows = jnp.concatenate([src[h, chunk, 0, pl.ds(0, HALF)], src[h, chunk, 1, pl.ds(0, HALF)]], axis=0)
        dot = lax.dot_general(tgt[quarter, pl.ds(0, 256)], rows, NT, preferred_element_type=f32)
        dot += jnp.dot(tgt_side[quarter], src_side[slot], preferred_element_type=f32)
        dot = dot * (COST_TO_BITS / 128.0)
        block[pl.ds(pl.multiple_of(quarter * 256, 256), 256), cols_of(h, chunk)] = dot
        peak[quarter, :, cols_of(h, chunk)] = jnp.max(dot.reshape(32, 8, 256), axis=0)

    def first_rows(h, chunk):
        top = jnp.max(jnp.max(peak[:, :, cols_of(h, chunk)], axis=0), axis=0, keepdims=True)

        def add(step, total):
            rows = pl.ds(pl.multiple_of(step * 256, 256), 256)
            values = jnp.exp2(block[rows, cols_of(h, chunk)] - top)
            return total + jnp.sum(values.reshape(8, 32, 256), axis=0)

        total = lax.fori_loop(0, ROWS // 256, add, jnp.zeros((32, 256), f32))
        s_msg[0, h, 0, pl.ds(chunk, 1)] = top + jnp.log2(jnp.sum(total, axis=0, keepdims=True))

    def whole_chunk(h, chunk):
        prepare_source(h, chunk, h)
        for quarter in range(QUARTERS):
            costs(quarter, h, chunk, h)
        first_rows(h, chunk)

    def chunk_at(k):
        return (y - k) % 4

    def take(h, k):
        ref = src.at[h, chunk_at(k), core]
        arrived(ref, 7 * h + k)
        started.append(send(ref, 7 * h + 3 + k, device(x, y, z, core + 1)))

    def exchange_s(turn, h):
        for dy, dc in s_peers:
            pltpu.make_async_remote_copy(
                src_ref=s_msg.at[turn, h, 0], dst_ref=s_msg.at[turn, h, dy * 2 + dc],
                send_sem=s_send.at[turn, h], recv_sem=s_recv.at[turn, h],
                device_id=device(x, y + dy, z, core + dc), device_id_type=MESH,
            ).start()

    def exchanged_s(turn, h):
        others = s_msg.at[turn, h, pl.ds(1, 7)]
        pltpu.make_async_copy(others, others, s_recv.at[turn, h]).wait()

    def exchange_t(turn):
        for dx, dz in t_peers:
            pltpu.make_async_remote_copy(
                src_ref=t_msg.at[turn, 0], dst_ref=t_msg.at[turn, dx * 4 + dz],
                send_sem=t_send.at[turn], recv_sem=t_recv.at[turn],
                device_id=device(x + dx, y, z + dz, core), device_id_type=MESH,
            ).start()
        others = t_msg.at[turn, pl.ds(1, 15)]
        pltpu.make_async_copy(others, others, t_recv.at[turn]).wait()

    away = 2 * (1 - z_lo)
    for quarter in range(2):
        prepare_target(2 * z_lo + quarter)
    for h in range(2):
        arrived(src.at[h, y, 1 - core], 7 * h)
        prepare_source(h, y, h)
        for quarter in range(2):
            costs(2 * z_lo + quarter, h, y, h)
    for quarter in range(2):
        arrived(tgt.at[away + quarter], 14 + quarter)
        prepare_target(away + quarter)
        for h in range(2):
            costs(away + quarter, h, y, h)
    for h in range(2):
        first_rows(h, y)
    for h in range(2):
        for k in (1, 3, 2):
            take(h, k)
        for k in (1, 3, 2):
            arrived(src.at[h, chunk_at(k), 1 - core], 7 * h + 3 + k)
            whole_chunk(h, chunk_at(k))
        exchange_s(0, h)

    source_count = COLS * 16.0
    target_count = ROWS * 8.0

    def joined(parts):
        top = jnp.max(parts, axis=0)
        return top + jnp.log2(jnp.sum(jnp.exp2(parts - top), axis=0))

    def spread_rows(h, values):
        for chunk in range(CHUNKS):
            first = (h * CHUNKS + chunk) * 256
            spread[:, first : first + 256] = jnp.broadcast_to(values[chunk : chunk + 1], (8, 256))

    def tile(l):
        return slice(l * LANES, (l + 1) * LANES)

    def tiles_of(h):
        return range(h * TILES // 2, (h + 1) * TILES // 2)

    def as_columns(values, b):
        return jnp.broadcast_to(values[b : b + 1], (LANES, LANES)).T

    def lane_reduced(op, ref, b):
        return op(ref[tile(b), :].T, axis=0, keepdims=True)

    def by_rows(step, count=8):
        return [pl.ds(pl.multiple_of((step * count + s) * 8, 8), 8) for s in range(count)]

    def first_columns(h):
        def find(step, _):
            for rows in by_rows(step):
                top = None
                for l in tiles_of(h):
                    value = block[rows, tile(l)] + spread[:, tile(l)]
                    top = value if top is None else jnp.maximum(top, value)
                partial[h, rows, :] = top
            return 0

        lax.fori_loop(0, ROWS // 64, find, 0)
        for b in range(8):
            top = lane_reduced(jnp.max, partial.at[h], b)
            top_dense[h, b : b + 1] = top
            col_max[h, tile(b), :] = jnp.broadcast_to(top, (LANES, LANES)).T

        def add(step, _):
            for rows in by_rows(step):
                top, total = col_max[h, rows, :], None
                for l in tiles_of(h):
                    value = jnp.exp2(block[rows, tile(l)] + (spread[:, tile(l)] - top))
                    plan[rows, tile(l)] = value
                    total = value if total is None else total + value
                partial[h, rows, :] = total
            return 0

        lax.fori_loop(0, ROWS // 64, add, 0)
        sums = [lane_reduced(jnp.sum, partial.at[h], b) for b in range(8)]
        return top_dense[h] + jnp.log2(jnp.concatenate(sums, axis=0))

    logs = []
    for h in range(2):
        exchanged_s(0, h)
        f_now = math.log2(target_count) - joined(s_msg[0, h])
        for c in range(2):
            f_first[h, c] = f_now[:, tile(c)]
        spread_rows(h, f_now)
        logs.append(first_columns(h))
    top = jnp.maximum(logs[0], logs[1])
    t_msg[0, 0] = top + jnp.log2(jnp.exp2(logs[0] - top) + jnp.exp2(logs[1] - top))
    pl.semaphore_wait(plane_sem, 3)
    exchange_t(0)
    g_now = math.log2(source_count) - joined(t_msg[0])
    g_first[...] = g_now
    scale = [jnp.exp2(top_dense[h] + g_now) for h in range(2)]
    for h in range(2):
        for b in range(8):
            weight[h, tile(b), :] = as_columns(scale[h], b)

    def row_sums(turn, h):
        def add(step, totals):
            for rows in by_rows(step):
                w = weight[h, rows, :]
                totals = tuple(total + plan[rows, tile(l)] * w for total, l in zip(totals, tiles_of(h)))
            return totals

        totals = lax.fori_loop(0, ROWS // 64, add, tuple(jnp.zeros((8, LANES), f32) for _ in tiles_of(h)))
        for i, total in enumerate(totals):
            s_msg[turn, h, 0, i // 2 : i // 2 + 1, tile(i % 2)] = jnp.sum(total, axis=0, keepdims=True)

    def column_sums(h):
        def add(step, _):
            for rows in by_rows(step):
                total = None
                for l in tiles_of(h):
                    value = plan[rows, tile(l)] * spread[:, tile(l)]
                    total = value if total is None else total + value
                partial[h, rows, :] = total
            return 0

        lax.fori_loop(0, ROWS // 64, add, 0)
        return jnp.concatenate([lane_reduced(jnp.sum, partial.at[h], b) for b in range(8)], axis=0)

    for turn in (1, 2):
        for h in range(2):
            row_sums(turn, h)
            exchange_s(turn, h)
        sums = 0.0
        for h in range(2):
            exchanged_s(turn, h)
            u_now = target_count / jnp.sum(s_msg[turn, h], axis=0)
            spread_rows(h, u_now)
            sums += scale[h] * column_sums(h)
            if turn == 2:
                for c in range(2):
                    f_first[h, c] = (f_first[h, c] + jnp.log2(u_now[:, tile(c)])) * (1.0 / COST_TO_BITS)
        t_msg[turn, 0] = sums
        exchange_t(turn)
        v_now = source_count / jnp.sum(t_msg[turn], axis=0)
        if turn == 1:
            for h in range(2):
                for b in range(8):
                    weight[h, tile(b), :] = as_columns(scale[h] * v_now, b)

    for h in range(2):
        f_out[h : h + 1] = f_first[h, core, pl.ds(y, 1)]
    g_first[...] = (g_first[...] + jnp.log2(v_now)) * (1.0 / COST_TO_BITS)
    g_out[...] = g_first[pl.ds(z_lo * 4, 4)]

    for copy in started:
        copy.wait_send()
    for turn in range(3):
        for h in range(2):
            others = s_msg.at[turn, h, pl.ds(1, 7)]
            pltpu.make_async_copy(others, others, s_send.at[turn, h]).wait()
        others = t_msg.at[turn, pl.ds(1, 15)]
        pltpu.make_async_copy(others, others, t_send.at[turn]).wait()


def body(source_embed, source_labels, target_embed, target_labels, label_table):
    vmem, hbm = pl.BlockSpec(memory_space=pltpu.VMEM), pl.BlockSpec(memory_space=pl.ANY)
    f32, bf16, dma = jnp.float32, jnp.bfloat16, pltpu.SemaphoreType.DMA
    f, g = pl.pallas_call(
        kernel,
        out_shape=(jax.ShapeDtypeStruct((2, HALF), f32), jax.ShapeDtypeStruct((4, LANES), f32)),
        in_specs=[hbm, vmem, hbm, vmem, vmem],
        out_specs=(vmem, vmem),
        scratch_shapes=[
            pltpu.VMEM((2, CHUNKS, 2, HALF + AUX, EMB), bf16),
            pltpu.VMEM((QUARTERS, 256 + AUX, EMB), bf16),
            pltpu.VMEM((2, LANES, 256), bf16),
            pltpu.VMEM((QUARTERS, 256, LANES), bf16),
            pltpu.VMEM((ROWS, COLS), f32),
            pltpu.VMEM((ROWS, COLS), f32),
            pltpu.VMEM((QUARTERS, 8, COLS), f32),
            pltpu.VMEM((2, ROWS, LANES), f32),
            pltpu.VMEM((2, ROWS, LANES), f32),
            pltpu.VMEM((2, ROWS, LANES), f32),
            pltpu.VMEM((8, COLS), f32),
            pltpu.VMEM((3, 2, 8, CHUNKS, 256), f32),
            pltpu.VMEM((3, 16, 8, LANES), f32),
            pltpu.VMEM((2, 2, CHUNKS, LANES), f32),
            pltpu.VMEM((2, 8, LANES), f32),
            pltpu.VMEM((8, LANES), f32),
            dma((4,)),
            dma((16,)),
            dma((16,)),
            dma((3, 2)),
            dma((3, 2)),
            dma((3,)),
            dma((3,)),
            pltpu.SemaphoreType.REGULAR,
        ],
        compiler_params=pltpu.CompilerParams(collective_id=0, has_side_effects=True, vmem_limit_bytes=40 << 20),
    )(
        source_embed,
        source_labels.reshape(1, SRC),
        target_embed,
        target_labels.reshape(1, TGT),
        label_table,
    )
    return f.reshape(SRC), g.reshape(TGT)


def solution(mesh):
    placed = (P(("dp", "stream"), None), P(("dp", "stream")), P("stream", None), P("stream"), P())
    return jax.shard_map(
        body,
        mesh=mesh,
        in_specs=placed,
        out_specs=(P(("dp", "stream")), P("stream")),
        check_vma=False,
    )
```

```python
import functools
import math

import jax
import jax.numpy as jnp
from jax import lax
from jax.experimental import pallas as pl
from jax.experimental.pallas import tpu as pltpu
from jax.sharding import PartitionSpec as P

MESH = pl.DeviceIdType.MESH
SCALE = 0.02
LOG2E = 1.0 / math.log(2.0)
COST_TO_BITS = LOG2E / SCALE

SRC = 256
HALF = 128
TGT = 512
EMB = 256
LABELS = 64
AUX = 16
CHUNKS = 4
QUARTERS = 4
ROWS = QUARTERS * 256
COLS = 2 * CHUNKS * 256
LANES = 128
TILES = COLS // LANES
NT = (((1,), (1,)), ((), ()))


def place():
    dp, stream = lax.axis_index("dp"), lax.axis_index("stream")
    div, rem = lax.div, lax.rem
    return div(dp, 2), div(stream, 4), rem(dp, 2) * 2 + rem(div(stream, 2), 2), rem(stream, 2)


def device(x, y, z, core):
    x, y, z, core = lax.rem(x, 4), lax.rem(y, 4), lax.rem(z, 4), lax.rem(core, 2)
    return (x * 2 + lax.div(z, 2), y * 4 + lax.rem(z, 2) * 2 + core)


def split3(value):
    high = value.astype(jnp.bfloat16).astype(jnp.float32)
    rest = value - high
    middle = rest.astype(jnp.bfloat16).astype(jnp.float32)
    return high, middle, rest - middle


def aux_rows(embed, labels):
    count = embed.shape[0]
    wide = embed.astype(jnp.float32)
    square = wide * wide
    high = square.astype(jnp.bfloat16)
    low = (square - high.astype(jnp.float32)).astype(jnp.bfloat16)
    ones = jnp.ones((AUX, EMB), jnp.bfloat16)
    norm = lax.dot_general(ones, high, NT, preferred_element_type=jnp.float32)
    norm += lax.dot_general(ones, low, NT, preferred_element_type=jnp.float32)
    first, second, third = split3(norm * (-128.0 / EMB))
    row = lax.broadcasted_iota(jnp.int32, (AUX, count), 0)
    marks = jnp.broadcast_to(labels.astype(jnp.float32), (AUX, count))
    out = jnp.where(row == 0, marks, 0.0)
    out = jnp.where(row == 1, first, out)
    out = jnp.where(row == 2, second, out)
    out = jnp.where(row == 3, third, out)
    return out.astype(jnp.bfloat16)


def kernel(
    src_ref, src_labels_ref, tgt_ref, tgt_labels_ref, table_ref, f_out, g_out,
    src_labels, tgt_labels, table, src, tgt, src_side, tgt_side, block, plan, peak, col_max, weight, weight_now, partial,
    spread, s_msg, t_msg, f_first, top_dense, g_first,
    in_sem, gather_send, gather_recv, s_send, s_recv, t_send, t_recv, plane_sem,
):
    x, y, z, core = place()
    z_lo = lax.rem(z, 2)
    s_peers = [(dy, dc) for dy in (2, 1, 3, 0) for dc in range(2) if (dy, dc) != (0, 0)]
    t_peers = [(dx, dz) for dx in (2, 1, 3, 0) for dz in (2, 1, 3, 0) if (dx, dz) != (0, 0)]
    f32 = jnp.float32

    near = [device(x, y + k, z, core) for k in (1, 2, 3)] + [device(x, y, z, core + 1)]
    near += [device(x, y, z + k, core) for k in (1, 2, 3)] + [device(x + k, y, z, core) for k in (1, 2, 3)]
    barrier = pltpu.get_barrier_semaphore()
    for target in near:
        pl.semaphore_signal(barrier, inc=1, device_id=target, device_id_type=MESH)

    loads = [
        pltpu.make_async_copy(
            src_ref.at[pl.ds(h * HALF, HALF)], src.at[h, y, core, pl.ds(0, HALF)], in_sem.at[h]
        )
        for h in range(2)
    ]
    loads += [
        pltpu.make_async_copy(
            tgt_ref.at[pl.ds(h * 256, 256)], tgt.at[2 * z_lo + h, pl.ds(0, 256)], in_sem.at[2 + h]
        )
        for h in range(2)
    ]
    loads += [
        pltpu.make_async_copy(src_labels_ref, src_labels, in_sem.at[4]),
        pltpu.make_async_copy(tgt_labels_ref, tgt_labels, in_sem.at[5]),
        pltpu.make_async_copy(table_ref, table, in_sem.at[6]),
    ]
    for load in loads:
        load.start()
    loads[4].wait()
    for h in range(2):
        loads[h].wait()
        src[h, y, core, pl.ds(HALF, AUX), 0:HALF] = aux_rows(
            src[h, y, core, pl.ds(0, HALF)], src_labels[:, h * HALF : (h + 1) * HALF]
        )
    loads[5].wait()
    for h in range(2):
        loads[2 + h].wait()
        tgt[2 * z_lo + h, pl.ds(256, AUX)] = aux_rows(
            tgt[2 * z_lo + h, pl.ds(0, 256)], tgt_labels[:, h * 256 : (h + 1) * 256]
        )

    pl.semaphore_wait(barrier, len(near))

    def send(ref, k, target):
        copy = pltpu.make_async_remote_copy(
            src_ref=ref, dst_ref=ref, send_sem=gather_send.at[k], recv_sem=gather_recv.at[k],
            device_id=target, device_id_type=MESH,
        )
        copy.start()
        return copy

    def arrived(ref, k):
        pltpu.make_async_copy(ref, ref, gather_recv.at[k]).wait()

    started = []
    for h in range(2):
        own = src.at[h, y, core]
        started += [send(own, 7 * h + k, device(x, y + k, z, core)) for k in (2, 1, 3)]
        started.append(send(own, 7 * h, device(x, y, z, core + 1)))
        if h == 0:
            started += [
                send(tgt.at[2 * z_lo + q], 14 + q, device(x, y, z + 1 + 2 * q, core)) for q in range(2)
            ]
    for k in (1, 2, 3):
        pl.semaphore_signal(plane_sem, inc=1, device_id=device(x + k, y, z, core), device_id_type=MESH)

    def cols_of(piece):
        h, chunk, c = piece
        return pl.ds(pl.multiple_of(((h * CHUNKS + chunk) * 2 + c) * HALF, HALF), HALF)

    def prepare_source(pieces, slot):
        aux = [src[h, chunk, c, pl.ds(HALF, AUX), 0:HALF].astype(f32) for h, chunk, c in pieces]
        aux = jnp.concatenate(aux, axis=1)
        row = lax.broadcasted_iota(jnp.int32, (LANES, 256), 0)
        side = jnp.where(row.astype(f32) == aux[0:1], 1.0, 0.0)
        side = jnp.where((row >= 67) & (row < 70), 1.0, side)
        for k in range(3):
            side = jnp.where(row == LABELS + k, aux[1 + k : 2 + k], side)
        src_side[slot] = side.astype(jnp.bfloat16)

    def prepare_target(quarter):
        aux = tgt[quarter, pl.ds(256, AUX)].astype(f32)
        row = lax.broadcasted_iota(jnp.int32, (LABELS, 256), 0)
        onehot = jnp.where(row.astype(f32) == aux[0:1], 1.0, 0.0).astype(jnp.bfloat16)
        costs = jnp.dot(table[...], onehot, preferred_element_type=f32) * -128.0
        rest = jnp.where(row < 3, 1.0, 0.0)
        for k in range(3):
            rest = jnp.where(row == 3 + k, aux[1 + k : 2 + k], rest)
        tgt_side[quarter] = jnp.concatenate([costs, rest], axis=0).T.astype(jnp.bfloat16)

    def costs(quarter, pieces, slot):
        rows = jnp.concatenate([src[h, chunk, c, pl.ds(0, HALF)] for h, chunk, c in pieces], axis=0)
        dot = lax.dot_general(tgt[quarter, pl.ds(0, 256)], rows, NT, preferred_element_type=f32)
        dot += jnp.dot(tgt_side[quarter], src_side[slot], preferred_element_type=f32)
        dot = dot * (COST_TO_BITS / 128.0)
        top = jnp.max(dot.reshape(32, 8, 256), axis=0)
        for i, piece in enumerate(pieces):
            at = slice(i * HALF, (i + 1) * HALF)
            block[pl.ds(pl.multiple_of(quarter * 256, 256), 256), cols_of(piece)] = dot[:, at]
            peak[quarter, :, cols_of(piece)] = top[:, at]

    def first_rows(pieces):
        tops = [jnp.max(jnp.max(peak[:, :, cols_of(p)], axis=0), axis=0, keepdims=True) for p in pieces]

        def add(step, totals):
            rows = pl.ds(pl.multiple_of(step * 256, 256), 256)
            values = [jnp.exp2(block[rows, cols_of(p)] - top) for p, top in zip(pieces, tops)]
            return tuple(t + jnp.sum(v.reshape(8, 32, HALF), axis=0) for t, v in zip(totals, values))

        totals = lax.fori_loop(0, ROWS // 256, add, (jnp.zeros((32, HALF), f32),) * 2)
        for (h, chunk, c), top, total in zip(pieces, tops, totals):
            s_msg[0, h, 0, c, pl.ds(chunk, 1)] = top + jnp.log2(jnp.sum(total, axis=0, keepdims=True))

    def whole(pieces):
        slot = pieces[0][0]
        prepare_source(pieces, slot)
        for quarter in range(QUARTERS):
            costs(quarter, pieces, slot)
        first_rows(pieces)

    def chunk_at(k):
        return lax.rem(y + 4 - k, 4)

    def take(h, k):
        ref = src.at[h, chunk_at(k), core]
        arrived(ref, 7 * h + k)
        started.append(send(ref, 7 * h + 3 + k, device(x, y, z, core + 1)))

    def exchange_s(turn, h):
        for dy, dc in s_peers:
            pltpu.make_async_remote_copy(
                src_ref=s_msg.at[turn, h, 0], dst_ref=s_msg.at[turn, h, dy * 2 + dc],
                send_sem=s_send.at[turn, h], recv_sem=s_recv.at[turn, h],
                device_id=device(x, y + dy, z, core + dc), device_id_type=MESH,
            ).start()

    def exchanged_s(turn, h):
        others = s_msg.at[turn, h, pl.ds(1, 7)]
        pltpu.make_async_copy(others, others, s_recv.at[turn, h]).wait()

    def exchange_t(turn):
        for dx, dz in t_peers:
            pltpu.make_async_remote_copy(
                src_ref=t_msg.at[turn, 0], dst_ref=t_msg.at[turn, dx * 4 + dz],
                send_sem=t_send.at[turn], recv_sem=t_recv.at[turn],
                device_id=device(x + dx, y, z + dz, core), device_id_type=MESH,
            ).start()
        others = t_msg.at[turn, pl.ds(1, 15)]
        pltpu.make_async_copy(others, others, t_recv.at[turn]).wait()

    away = 2 * (1 - z_lo)
    own = [[(h, y, c) for c in range(2)] for h in range(2)]
    loads[6].wait()
    for quarter in range(2):
        prepare_target(2 * z_lo + quarter)
    for h in range(2):
        arrived(src.at[h, y, 1 - core], 7 * h)
        prepare_source(own[h], h)
        for quarter in range(2):
            costs(2 * z_lo + quarter, own[h], h)
    for quarter in range(2):
        arrived(tgt.at[away + quarter], 14 + quarter)
        prepare_target(away + quarter)
        for h in range(2):
            costs(away + quarter, own[h], h)
    for h in range(2):
        first_rows(own[h])
    for h in range(2):
        for k in (1, 3, 2):
            take(h, k)
        whole([(h, chunk_at(1), core), (h, chunk_at(3), core)])
        other = 1 - core
        arrived(src.at[h, chunk_at(1), other], 7 * h + 4)
        whole([(h, chunk_at(2), core), (h, chunk_at(1), other)])
        arrived(src.at[h, chunk_at(3), other], 7 * h + 6)
        arrived(src.at[h, chunk_at(2), other], 7 * h + 5)
        whole([(h, chunk_at(3), other), (h, chunk_at(2), other)])
        exchange_s(0, h)

    source_count = COLS * 16.0
    target_count = ROWS * 8.0

    def joined(parts):
        top = jnp.max(parts, axis=0)
        return top + jnp.log2(jnp.sum(jnp.exp2(parts - top), axis=0))

    def spread_rows(h, values):
        for i in range(2 * CHUNKS):
            spread[:, tile(h * 2 * CHUNKS + i)] = jnp.broadcast_to(values[i % 2, i // 2 : i // 2 + 1], (8, HALF))

    def tile(l):
        return slice(l * LANES, (l + 1) * LANES)

    def tiles_of(h):
        return range(h * TILES // 2, (h + 1) * TILES // 2)

    def as_columns(values, b):
        return jnp.broadcast_to(values[b : b + 1], (LANES, LANES)).T

    def lane_reduced(op, ref, b):
        return op(ref[tile(b), :].T, axis=0, keepdims=True)

    def by_rows(step, count=8):
        return [pl.ds(pl.multiple_of((step * count + s) * 8, 8), 8) for s in range(count)]

    def first_columns(h):
        across = [spread[:, tile(l)] for l in tiles_of(h)]

        def find(step, _):
            for rows in by_rows(step):
                top = None
                for l, given in zip(tiles_of(h), across):
                    value = block[rows, tile(l)] + given
                    top = value if top is None else jnp.maximum(top, value)
                partial[h, rows, :] = top
            return 0

        lax.fori_loop(0, ROWS // 64, find, 0)
        for b in range(8):
            top = lane_reduced(jnp.max, partial.at[h], b)
            top_dense[h, b : b + 1] = top
            col_max[h, tile(b), :] = jnp.broadcast_to(top, (LANES, LANES)).T

        def add(step, _):
            for rows in by_rows(step):
                top, total = col_max[h, rows, :], None
                for l, given in zip(tiles_of(h), across):
                    value = jnp.exp2(block[rows, tile(l)] + (given - top))
                    plan[rows, tile(l)] = value
                    total = value if total is None else total + value
                partial[h, rows, :] = total
            return 0

        lax.fori_loop(0, ROWS // 64, add, 0)
        sums = [lane_reduced(jnp.sum, partial.at[h], b) for b in range(8)]
        return top_dense[h] + jnp.log2(jnp.concatenate(sums, axis=0))

    logs = []
    for h in range(2):
        exchanged_s(0, h)
        f_now = math.log2(target_count) - joined(s_msg[0, h])
        f_first[h] = f_now
        spread_rows(h, f_now)
        logs.append(first_columns(h))
    top = jnp.maximum(logs[0], logs[1])
    t_msg[0, 0] = top + jnp.log2(jnp.exp2(logs[0] - top) + jnp.exp2(logs[1] - top))
    pl.semaphore_wait(plane_sem, 3)
    exchange_t(0)
    g_now = math.log2(source_count) - joined(t_msg[0])
    g_first[...] = g_now
    for h in range(2):
        scale = jnp.exp2(top_dense[h] + g_now)
        for b in range(8):
            weight[h, tile(b), :] = as_columns(scale, b)

    def row_sums(turn, h):
        def add(step, totals):
            for rows in by_rows(step):
                w = (weight if turn == 1 else weight_now)[h, rows, :]
                totals = tuple(total + plan[rows, tile(l)] * w for total, l in zip(totals, tiles_of(h)))
            return totals

        totals = lax.fori_loop(0, ROWS // 64, add, tuple(jnp.zeros((8, LANES), f32) for _ in tiles_of(h)))
        for i, total in enumerate(totals):
            s_msg[turn, h, 0, i % 2, i // 2 : i // 2 + 1] = jnp.sum(total, axis=0, keepdims=True)

    def column_sums(h):
        across = [spread[:, tile(l)] for l in tiles_of(h)]

        def add(step, _):
            for rows in by_rows(step):
                total = None
                for l, given in zip(tiles_of(h), across):
                    value = plan[rows, tile(l)] * given
                    total = value if total is None else total + value
                total = total * weight[h, rows, :]
                partial[0, rows, :] = total if h == 0 else total + partial[0, rows, :]
            return 0

        lax.fori_loop(0, ROWS // 64, add, 0)

    for turn in (1, 2):
        for h in range(2):
            row_sums(turn, h)
            exchange_s(turn, h)
        for h in range(2):
            exchanged_s(turn, h)
            u_now = target_count / jnp.sum(s_msg[turn, h], axis=0)
            spread_rows(h, u_now)
            column_sums(h)
            if turn == 2:
                f_first[h] = (f_first[h] + jnp.log2(u_now)) * (1.0 / COST_TO_BITS)
        for b in range(8):
            t_msg[turn, 0, b : b + 1] = lane_reduced(jnp.sum, partial.at[0], b)
        exchange_t(turn)
        v_now = source_count / jnp.sum(t_msg[turn], axis=0)
        if turn == 1:
            for b in range(8):
                column = as_columns(v_now, b)
                for h in range(2):
                    weight_now[h, tile(b), :] = weight[h, tile(b), :] * column

    for h in range(2):
        f_out[h : h + 1] = f_first[h, core, pl.ds(y, 1)]
    g_first[...] = (g_first[...] + jnp.log2(v_now)) * (1.0 / COST_TO_BITS)
    g_out[...] = g_first[pl.ds(z_lo * 4, 4)]

    for copy in started:
        copy.wait_send()
    for turn in range(3):
        for h in range(2):
            others = s_msg.at[turn, h, pl.ds(1, 7)]
            pltpu.make_async_copy(others, others, s_send.at[turn, h]).wait()
        others = t_msg.at[turn, pl.ds(1, 15)]
        pltpu.make_async_copy(others, others, t_send.at[turn]).wait()


def hand_on(f_ref, g_ref, f_out, g_out):
    f_out[...] = f_ref[...]
    g_out[...] = g_ref[...]


def body(source_embed, source_labels, target_embed, target_labels, label_table):
    vmem, hbm = pl.BlockSpec(memory_space=pltpu.VMEM), pl.BlockSpec(memory_space=pltpu.HBM)
    f32, bf16, dma = jnp.float32, jnp.bfloat16, pltpu.SemaphoreType.DMA
    f, g = pl.pallas_call(
        kernel,
        out_shape=(jax.ShapeDtypeStruct((2, HALF), f32), jax.ShapeDtypeStruct((4, LANES), f32)),
        in_specs=[hbm] * 5,
        out_specs=(vmem, vmem),
        scratch_shapes=[
            pltpu.VMEM((1, SRC), jnp.int32),
            pltpu.VMEM((1, TGT), jnp.int32),
            pltpu.VMEM((LABELS, LABELS), bf16),
            pltpu.VMEM((2, CHUNKS, 2, HALF + AUX, EMB), bf16),
            pltpu.VMEM((QUARTERS, 256 + AUX, EMB), bf16),
            pltpu.VMEM((2, LANES, 256), bf16),
            pltpu.VMEM((QUARTERS, 256, LANES), bf16),
            pltpu.VMEM((ROWS, COLS), f32),
            pltpu.VMEM((ROWS, COLS), f32),
            pltpu.VMEM((QUARTERS, 8, COLS), f32),
            pltpu.VMEM((2, ROWS, LANES), f32),
            pltpu.VMEM((2, ROWS, LANES), f32),
            pltpu.VMEM((2, ROWS, LANES), f32),
            pltpu.VMEM((2, ROWS, LANES), f32),
            pltpu.VMEM((8, COLS), f32),
            pltpu.VMEM((3, 2, 8, 2, CHUNKS, LANES), f32),
            pltpu.VMEM((3, 16, 8, LANES), f32),
            pltpu.VMEM((2, 2, CHUNKS, LANES), f32),
            pltpu.VMEM((2, 8, LANES), f32),
            pltpu.VMEM((8, LANES), f32),
            dma((7,)),
            dma((16,)),
            dma((16,)),
            dma((3, 2)),
            dma((3, 2)),
            dma((3,)),
            dma((3,)),
            pltpu.SemaphoreType.REGULAR,
        ],
        compiler_params=pltpu.CompilerParams(collective_id=0, has_side_effects=True, vmem_limit_bytes=60 << 20),
    )(
        source_embed,
        source_labels.reshape(1, SRC),
        target_embed,
        target_labels.reshape(1, TGT),
        label_table,
    )
    f, g = pl.pallas_call(
        hand_on,
        out_shape=(jax.ShapeDtypeStruct((2, HALF), f32), jax.ShapeDtypeStruct((4, LANES), f32)),
        in_specs=[vmem] * 2,
        out_specs=(vmem, vmem),
    )(f, g)
    return f.reshape(SRC), g.reshape(TGT)


def solution(mesh):
    placed = (P(("dp", "stream"), None), P(("dp", "stream")), P("stream", None), P("stream"), P())
    return jax.shard_map(
        body,
        mesh=mesh,
        in_specs=placed,
        out_specs=(P(("dp", "stream")), P("stream")),
        check_vma=False,
    )
```

```python
import functools
import math

import jax
import jax.numpy as jnp
from jax import lax
from jax.experimental import pallas as pl
from jax.experimental.pallas import tpu as pltpu
from jax.sharding import PartitionSpec as P

MESH = pl.DeviceIdType.MESH
SCALE = 0.02
LOG2E = 1.0 / math.log(2.0)
COST_TO_BITS = LOG2E / SCALE

SRC = 256
HALF = 128
TGT = 512
EMB = 256
LABELS = 64
AUX = 16
CHUNKS = 4
QUARTERS = 4
ROWS = QUARTERS * 256
COLS = 2 * CHUNKS * 256
LANES = 128
TILES = COLS // LANES
NT = (((1,), (1,)), ((), ()))


def place():
    dp, stream = lax.axis_index("dp"), lax.axis_index("stream")
    div, rem = lax.div, lax.rem
    return div(dp, 2), div(stream, 4), rem(dp, 2) * 2 + rem(div(stream, 2), 2), rem(stream, 2)


def device(x, y, z, core):
    x, y, z, core = lax.rem(x, 4), lax.rem(y, 4), lax.rem(z, 4), lax.rem(core, 2)
    return (x * 2 + lax.div(z, 2), y * 4 + lax.rem(z, 2) * 2 + core)


def split3(value):
    high = value.astype(jnp.bfloat16).astype(jnp.float32)
    rest = value - high
    middle = rest.astype(jnp.bfloat16).astype(jnp.float32)
    return high, middle, rest - middle


def aux_rows(embed, labels):
    count = embed.shape[0]
    wide = embed.astype(jnp.float32)
    square = wide * wide
    high = square.astype(jnp.bfloat16)
    low = (square - high.astype(jnp.float32)).astype(jnp.bfloat16)
    ones = jnp.ones((AUX, EMB), jnp.bfloat16)
    norm = lax.dot_general(ones, high, NT, preferred_element_type=jnp.float32)
    norm += lax.dot_general(ones, low, NT, preferred_element_type=jnp.float32)
    first, second, third = split3(norm * (-128.0 / EMB))
    row = lax.broadcasted_iota(jnp.int32, (AUX, count), 0)
    marks = jnp.broadcast_to(labels.astype(jnp.float32), (AUX, count))
    out = jnp.where(row == 0, marks, 0.0)
    out = jnp.where(row == 1, first, out)
    out = jnp.where(row == 2, second, out)
    out = jnp.where(row == 3, third, out)
    return out.astype(jnp.bfloat16)


def kernel(
    src_ref, src_labels_ref, tgt_ref, tgt_labels_ref, table_ref, f_out, g_out,
    src_labels, tgt_labels, table, src, tgt, src_side, tgt_side, block, plan, peak, col_max, weight, partial,
    spread, s_msg, t_msg, f_first, top_dense, g_first,
    in_sem, gather_send, gather_recv, s_send, s_recv, t_send, t_recv, plane_sem,
):
    x, y, z, core = place()
    z_lo = lax.rem(z, 2)
    s_peers = [(dy, dc) for dy in (2, 1, 3, 0) for dc in range(2) if (dy, dc) != (0, 0)]
    t_peers = [(dx, dz) for dx in (2, 1, 3, 0) for dz in (2, 1, 3, 0) if (dx, dz) != (0, 0)]
    f32 = jnp.float32

    near = [device(x, y + k, z, core) for k in (1, 2, 3)] + [device(x, y, z, core + 1)]
    near += [device(x, y, z + k, core) for k in (1, 2, 3)] + [device(x + k, y, z, core) for k in (1, 2, 3)]
    barrier = pltpu.get_barrier_semaphore()
    for target in near:
        pl.semaphore_signal(barrier, inc=1, device_id=target, device_id_type=MESH)

    loads = [
        pltpu.make_async_copy(
            src_ref.at[pl.ds(h * HALF, HALF)], src.at[h, y, core, pl.ds(0, HALF)], in_sem.at[h]
        )
        for h in range(2)
    ]
    loads += [
        pltpu.make_async_copy(
            tgt_ref.at[pl.ds(h * 256, 256)], tgt.at[2 * z_lo + h, pl.ds(0, 256)], in_sem.at[2 + h]
        )
        for h in range(2)
    ]
    loads += [
        pltpu.make_async_copy(src_labels_ref, src_labels, in_sem.at[4]),
        pltpu.make_async_copy(tgt_labels_ref, tgt_labels, in_sem.at[5]),
        pltpu.make_async_copy(table_ref, table, in_sem.at[6]),
    ]
    for load in loads:
        load.start()
    loads[4].wait()
    for h in range(2):
        loads[h].wait()
        src[h, y, core, pl.ds(HALF, AUX), 0:HALF] = aux_rows(
            src[h, y, core, pl.ds(0, HALF)], src_labels[:, h * HALF : (h + 1) * HALF]
        )
    loads[5].wait()
    for h in range(2):
        loads[2 + h].wait()
        tgt[2 * z_lo + h, pl.ds(256, AUX)] = aux_rows(
            tgt[2 * z_lo + h, pl.ds(0, 256)], tgt_labels[:, h * 256 : (h + 1) * 256]
        )

    pl.semaphore_wait(barrier, len(near))

    def send(ref, k, target):
        copy = pltpu.make_async_remote_copy(
            src_ref=ref, dst_ref=ref, send_sem=gather_send.at[k], recv_sem=gather_recv.at[k],
            device_id=target, device_id_type=MESH,
        )
        copy.start()
        return copy

    def arrived(ref, k):
        pltpu.make_async_copy(ref, ref, gather_recv.at[k]).wait()

    started = []
    for h in range(2):
        own = src.at[h, y, core]
        started += [send(own, 7 * h + k, device(x, y + k, z, core)) for k in (2, 1, 3)]
        started.append(send(own, 7 * h, device(x, y, z, core + 1)))
        if h == 0:
            started += [
                send(tgt.at[2 * z_lo + q], 14 + q, device(x, y, z + 1 + 2 * q, core)) for q in range(2)
            ]
    for k in (1, 2, 3):
        pl.semaphore_signal(plane_sem, inc=1, device_id=device(x + k, y, z, core), device_id_type=MESH)

    def cols_of(piece):
        h, chunk, c = piece
        return pl.ds(pl.multiple_of(((h * CHUNKS + chunk) * 2 + c) * HALF, HALF), HALF)

    def prepare_source(pieces, slot):
        aux = [src[h, chunk, c, pl.ds(HALF, AUX), 0:HALF].astype(f32) for h, chunk, c in pieces]
        aux = jnp.concatenate(aux, axis=1)
        row = lax.broadcasted_iota(jnp.int32, (LANES, 256), 0)
        side = jnp.where(row.astype(f32) == aux[0:1], 1.0, 0.0)
        side = jnp.where((row >= 67) & (row < 70), 1.0, side)
        for k in range(3):
            side = jnp.where(row == LABELS + k, aux[1 + k : 2 + k], side)
        src_side[slot] = side.astype(jnp.bfloat16)

    def prepare_target(quarter):
        aux = tgt[quarter, pl.ds(256, AUX)].astype(f32)
        row = lax.broadcasted_iota(jnp.int32, (LABELS, 256), 0)
        onehot = jnp.where(row.astype(f32) == aux[0:1], 1.0, 0.0).astype(jnp.bfloat16)
        costs = jnp.dot(table[...], onehot, preferred_element_type=f32) * -128.0
        rest = jnp.where(row < 3, 1.0, 0.0)
        for k in range(3):
            rest = jnp.where(row == 3 + k, aux[1 + k : 2 + k], rest)
        tgt_side[quarter] = jnp.concatenate([costs, rest], axis=0).T.astype(jnp.bfloat16)

    def costs(quarter, pieces, slot):
        rows = jnp.concatenate([src[h, chunk, c, pl.ds(0, HALF)] for h, chunk, c in pieces], axis=0)
        dot = lax.dot_general(tgt[quarter, pl.ds(0, 256)], rows, NT, preferred_element_type=f32)
        dot += jnp.dot(tgt_side[quarter], src_side[slot], preferred_element_type=f32)
        dot = dot * (COST_TO_BITS / 128.0)
        top = jnp.max(dot.reshape(32, 8, 256), axis=0)
        for i, piece in enumerate(pieces):
            at = slice(i * HALF, (i + 1) * HALF)
            block[pl.ds(pl.multiple_of(quarter * 256, 256), 256), cols_of(piece)] = dot[:, at]
            peak[quarter, :, cols_of(piece)] = top[:, at]

    def first_rows(pieces):
        tops = [jnp.max(jnp.max(peak[:, :, cols_of(p)], axis=0), axis=0, keepdims=True) for p in pieces]

        def add(step, totals):
            rows = pl.ds(pl.multiple_of(step * 256, 256), 256)
            values = [jnp.exp2(block[rows, cols_of(p)] - top) for p, top in zip(pieces, tops)]
            return tuple(t + jnp.sum(v.reshape(8, 32, HALF), axis=0) for t, v in zip(totals, values))

        totals = lax.fori_loop(0, ROWS // 256, add, (jnp.zeros((32, HALF), f32),) * 2)
        for (h, chunk, c), top, total in zip(pieces, tops, totals):
            s_msg[0, h, 0, c, pl.ds(chunk, 1)] = top + jnp.log2(jnp.sum(total, axis=0, keepdims=True))

    def whole(pieces):
        slot = pieces[0][0]
        prepare_source(pieces, slot)
        for quarter in range(QUARTERS):
            costs(quarter, pieces, slot)
        first_rows(pieces)

    def chunk_at(k):
        return lax.rem(y + 4 - k, 4)

    def take(h, k):
        ref = src.at[h, chunk_at(k), core]
        arrived(ref, 7 * h + k)
        started.append(send(ref, 7 * h + 3 + k, device(x, y, z, core + 1)))

    def exchange_s(turn, h):
        for dy, dc in s_peers:
            pltpu.make_async_remote_copy(
                src_ref=s_msg.at[turn, h, 0], dst_ref=s_msg.at[turn, h, dy * 2 + dc],
                send_sem=s_send.at[turn, h], recv_sem=s_recv.at[turn, h],
                device_id=device(x, y + dy, z, core + dc), device_id_type=MESH,
            ).start()

    def exchanged_s(turn, h):
        others = s_msg.at[turn, h, pl.ds(1, 7)]
        pltpu.make_async_copy(others, others, s_recv.at[turn, h]).wait()

    def send_t(turn):
        for dx, dz in t_peers:
            pltpu.make_async_remote_copy(
                src_ref=t_msg.at[turn, 0], dst_ref=t_msg.at[turn, dx * 4 + dz],
                send_sem=t_send.at[turn], recv_sem=t_recv.at[turn],
                device_id=device(x + dx, y, z + dz, core), device_id_type=MESH,
            ).start()

    def received_t(turn):
        others = t_msg.at[turn, pl.ds(1, 15)]
        pltpu.make_async_copy(others, others, t_recv.at[turn]).wait()

    away = 2 * (1 - z_lo)
    own = [[(h, y, c) for c in range(2)] for h in range(2)]
    loads[6].wait()
    for quarter in range(2):
        prepare_target(2 * z_lo + quarter)
    for h in range(2):
        arrived(src.at[h, y, 1 - core], 7 * h)
        prepare_source(own[h], h)
        for quarter in range(2):
            costs(2 * z_lo + quarter, own[h], h)
    for quarter in range(2):
        arrived(tgt.at[away + quarter], 14 + quarter)
        prepare_target(away + quarter)
        for h in range(2):
            costs(away + quarter, own[h], h)
    for h in range(2):
        first_rows(own[h])
    for h in range(2):
        for k in (1, 3, 2):
            take(h, k)
        whole([(h, chunk_at(1), core), (h, chunk_at(3), core)])
        other = 1 - core
        arrived(src.at[h, chunk_at(1), other], 7 * h + 4)
        whole([(h, chunk_at(2), core), (h, chunk_at(1), other)])
        arrived(src.at[h, chunk_at(3), other], 7 * h + 6)
        arrived(src.at[h, chunk_at(2), other], 7 * h + 5)
        whole([(h, chunk_at(3), other), (h, chunk_at(2), other)])
        exchange_s(0, h)

    source_count = COLS * 16.0
    target_count = ROWS * 8.0

    def joined(parts):
        top = jnp.max(parts, axis=0)
        return top + jnp.log2(jnp.sum(jnp.exp2(parts - top), axis=0))

    def spread_rows(h, values):
        for i in range(2 * CHUNKS):
            spread[:, tile(h * 2 * CHUNKS + i)] = jnp.broadcast_to(values[i % 2, i // 2 : i // 2 + 1], (8, HALF))

    def tile(l):
        return slice(l * LANES, (l + 1) * LANES)

    def tiles_of(h):
        return range(h * TILES // 2, (h + 1) * TILES // 2)

    def as_columns(values, b):
        return jnp.broadcast_to(values[b : b + 1], (LANES, LANES)).T

    def rows_in(b):
        return [slice(b * LANES + i * 8, b * LANES + i * 8 + 8) for i in range(LANES // 8)]

    def lane_reduced(op, tiles):
        return op(jnp.concatenate(tiles, axis=0).T, axis=0, keepdims=True)

    def first_columns(h):
        across = [spread[:, tile(l)] for l in tiles_of(h)]
        logs = []
        for b in range(8):
            tops = []
            for rows in rows_in(b):
                top = None
                for l, given in zip(tiles_of(h), across):
                    value = block[rows, tile(l)] + given
                    top = value if top is None else jnp.maximum(top, value)
                tops.append(top)
            top = lane_reduced(jnp.max, tops)
            top_dense[h, b : b + 1] = top
            col_max[h, tile(b), :] = jnp.broadcast_to(top, (LANES, LANES)).T
        for b in range(8):
            totals = []
            for rows in rows_in(b):
                top_column, total = col_max[h, rows, :], None
                for l, given in zip(tiles_of(h), across):
                    value = jnp.exp2(block[rows, tile(l)] + (given - top_column))
                    plan[rows, tile(l)] = value
                    total = value if total is None else total + value
                totals.append(total)
            logs.append(jnp.log2(lane_reduced(jnp.sum, totals)))
        return top_dense[h] + jnp.concatenate(logs, axis=0)

    logs = []
    for h in range(2):
        exchanged_s(0, h)
        f_now = math.log2(target_count) - joined(s_msg[0, h])
        f_first[h] = f_now
        spread_rows(h, f_now)
        logs.append(first_columns(h))
    top = jnp.maximum(logs[0], logs[1])
    t_msg[0, 0] = top + jnp.log2(jnp.exp2(logs[0] - top) + jnp.exp2(logs[1] - top))
    pl.semaphore_wait(plane_sem, 3)
    send_t(0)

    def rescale(step, _):
        for s in range(8):
            rows = pl.ds(pl.multiple_of(step * 64 + s * 8, 8), 8)
            both = jnp.maximum(col_max[0, rows, :], col_max[1, rows, :])
            for h in range(2):
                down = jnp.exp2(col_max[h, rows, :] - both)
                for l in tiles_of(h):
                    block[rows, tile(l)] = plan[rows, tile(l)] * down
        return 0

    lax.fori_loop(0, ROWS // 64, rescale, 0)
    top = jnp.maximum(top_dense[0], top_dense[1])
    received_t(0)
    g_now = math.log2(source_count) - joined(t_msg[0])
    g_first[...] = g_now
    scale = jnp.exp2(top + g_now)
    def row_sums(turn, h, factors):
        totals = [None for _ in tiles_of(h)]
        for b in range(8):
            if h == 0:
                weight[tile(b), :] = as_columns(factors, b)
            for rows in rows_in(b):
                w = weight[rows, :]
                values = [block[rows, tile(l)] * w for l in tiles_of(h)]
                totals = [v if t is None else t + v for t, v in zip(totals, values)]
        for i, total in enumerate(totals):
            s_msg[turn, h, 0, i % 2, i // 2 : i // 2 + 1] = jnp.sum(total, axis=0, keepdims=True)

    def column_sums(h, b, across):
        totals = []
        for rows in rows_in(b):
            total = None if h == 0 else partial[rows, :]
            for l, given in zip(tiles_of(h), across):
                value = block[rows, tile(l)] * given
                total = value if total is None else total + value
            if h == 0:
                partial[rows, :] = total
            totals.append(total)
        return totals

    factors = scale
    for turn in (1, 2):
        for h in range(2):
            row_sums(turn, h, factors)
            exchange_s(turn, h)
        sums = []
        for h in range(2):
            exchanged_s(turn, h)
            u_now = target_count / jnp.sum(s_msg[turn, h], axis=0)
            spread_rows(h, u_now)
            across = [spread[:, tile(l)] for l in tiles_of(h)]
            for b in range(8):
                totals = column_sums(h, b, across)
                if h == 1:
                    sums.append(lane_reduced(jnp.sum, totals))
            if turn == 2:
                f_first[h] = (f_first[h] + jnp.log2(u_now)) * (1.0 / COST_TO_BITS)
        t_msg[turn, 0] = scale * jnp.concatenate(sums, axis=0)
        send_t(turn)
        received_t(turn)
        v_now = source_count / jnp.sum(t_msg[turn], axis=0)
        factors = scale * v_now

    for h in range(2):
        f_out[h : h + 1] = f_first[h, core, pl.ds(y, 1)]
    g_first[...] = (g_first[...] + jnp.log2(v_now)) * (1.0 / COST_TO_BITS)
    g_out[...] = g_first[pl.ds(z_lo * 4, 4)]

    for copy in started:
        copy.wait_send()
    for turn in range(3):
        for h in range(2):
            others = s_msg.at[turn, h, pl.ds(1, 7)]
            pltpu.make_async_copy(others, others, s_send.at[turn, h]).wait()
        others = t_msg.at[turn, pl.ds(1, 15)]
        pltpu.make_async_copy(others, others, t_send.at[turn]).wait()


def hand_on(f_ref, g_ref, f_out, g_out):
    f_out[...] = f_ref[...]
    g_out[...] = g_ref[...]


def body(source_embed, source_labels, target_embed, target_labels, label_table):
    vmem, hbm = pl.BlockSpec(memory_space=pltpu.VMEM), pl.BlockSpec(memory_space=pltpu.HBM)
    f32, bf16, dma = jnp.float32, jnp.bfloat16, pltpu.SemaphoreType.DMA
    f, g = pl.pallas_call(
        kernel,
        out_shape=(jax.ShapeDtypeStruct((2, HALF), f32), jax.ShapeDtypeStruct((4, LANES), f32)),
        in_specs=[hbm] * 5,
        out_specs=(vmem, vmem),
        scratch_shapes=[
            pltpu.VMEM((1, SRC), jnp.int32),
            pltpu.VMEM((1, TGT), jnp.int32),
            pltpu.VMEM((LABELS, LABELS), bf16),
            pltpu.VMEM((2, CHUNKS, 2, HALF + AUX, EMB), bf16),
            pltpu.VMEM((QUARTERS, 256 + AUX, EMB), bf16),
            pltpu.VMEM((2, LANES, 256), bf16),
            pltpu.VMEM((QUARTERS, 256, LANES), bf16),
            pltpu.VMEM((ROWS, COLS), f32),
            pltpu.VMEM((ROWS, COLS), f32),
            pltpu.VMEM((QUARTERS, 8, COLS), f32),
            pltpu.VMEM((2, ROWS, LANES), f32),
            pltpu.VMEM((ROWS, LANES), f32),
            pltpu.VMEM((ROWS, LANES), f32),
            pltpu.VMEM((8, COLS), f32),
            pltpu.VMEM((3, 2, 8, 2, CHUNKS, LANES), f32),
            pltpu.VMEM((3, 16, 8, LANES), f32),
            pltpu.VMEM((2, 2, CHUNKS, LANES), f32),
            pltpu.VMEM((2, 8, LANES), f32),
            pltpu.VMEM((8, LANES), f32),
            dma((7,)),
            dma((16,)),
            dma((16,)),
            dma((3, 2)),
            dma((3, 2)),
            dma((3,)),
            dma((3,)),
            pltpu.SemaphoreType.REGULAR,
        ],
        compiler_params=pltpu.CompilerParams(collective_id=0, has_side_effects=True, vmem_limit_bytes=60 << 20),
    )(
        source_embed,
        source_labels.reshape(1, SRC),
        target_embed,
        target_labels.reshape(1, TGT),
        label_table,
    )
    f, g = pl.pallas_call(
        hand_on,
        out_shape=(jax.ShapeDtypeStruct((2, HALF), f32), jax.ShapeDtypeStruct((4, LANES), f32)),
        in_specs=[vmem] * 2,
        out_specs=(vmem, vmem),
    )(f, g)
    return f.reshape(SRC), g.reshape(TGT)


def solution(mesh):
    placed = (P(("dp", "stream"), None), P(("dp", "stream")), P("stream", None), P("stream"), P())
    return jax.shard_map(
        body,
        mesh=mesh,
        in_specs=placed,
        out_specs=(P(("dp", "stream")), P("stream")),
        check_vma=False,
    )
```

```python
import functools
import math

import jax
import jax.numpy as jnp
from jax import lax
from jax.experimental import pallas as pl
from jax.experimental.pallas import tpu as pltpu
from jax.sharding import PartitionSpec as P

MESH = pl.DeviceIdType.MESH
SCALE = 0.02
LOG2E = 1.0 / math.log(2.0)
COST_TO_BITS = LOG2E / SCALE

SRC = 256
HALF = 128
TGT = 512
EMB = 256
LABELS = 64
AUX = 16
CHUNKS = 4
QUARTERS = 4
ROWS = QUARTERS * 256
COLS = 2 * CHUNKS * 256
LANES = 128
TILES = COLS // LANES
NT = (((1,), (1,)), ((), ()))


def place():
    dp, stream = lax.axis_index("dp"), lax.axis_index("stream")
    div, rem = lax.div, lax.rem
    return div(dp, 2), div(stream, 4), rem(dp, 2) * 2 + rem(div(stream, 2), 2), rem(stream, 2)


def device(x, y, z, core):
    x, y, z, core = lax.rem(x, 4), lax.rem(y, 4), lax.rem(z, 4), lax.rem(core, 2)
    return (x * 2 + lax.div(z, 2), y * 4 + lax.rem(z, 2) * 2 + core)


def split3(value):
    high = value.astype(jnp.bfloat16).astype(jnp.float32)
    rest = value - high
    middle = rest.astype(jnp.bfloat16).astype(jnp.float32)
    return high, middle, rest - middle


def aux_rows(embed, labels):
    count = embed.shape[0]
    wide = embed.astype(jnp.float32)
    square = wide * wide
    high = square.astype(jnp.bfloat16)
    low = (square - high.astype(jnp.float32)).astype(jnp.bfloat16)
    ones = jnp.ones((AUX, EMB), jnp.bfloat16)
    norm = lax.dot_general(ones, high, NT, preferred_element_type=jnp.float32)
    norm += lax.dot_general(ones, low, NT, preferred_element_type=jnp.float32)
    first, second, third = split3(norm * (-128.0 / EMB))
    row = lax.broadcasted_iota(jnp.int32, (AUX, count), 0)
    marks = jnp.broadcast_to(labels.astype(jnp.float32), (AUX, count))
    out = jnp.where(row == 0, marks, 0.0)
    out = jnp.where(row == 1, first, out)
    out = jnp.where(row == 2, second, out)
    out = jnp.where(row == 3, third, out)
    return out.astype(jnp.bfloat16)


def kernel(
    src_ref, src_labels_ref, tgt_ref, tgt_labels_ref, table_ref, out,
    src_labels, tgt_labels, table, src, tgt, src_side, tgt_side, block, plan, peak, col_max, weight, partial,
    spread, s_msg, t_msg, f_first, top_dense, g_first,
    in_sem, gather_send, gather_recv, s_send, s_recv, t_send, t_recv, plane_sem,
):
    x, y, z, core = place()
    z_lo = lax.rem(z, 2)
    s_peers = [(dy, dc) for dy in (2, 1, 3, 0) for dc in range(2) if (dy, dc) != (0, 0)]
    t_peers = [(dx, dz) for dx in (2, 1, 3, 0) for dz in (2, 1, 3, 0) if (dx, dz) != (0, 0)]
    f32 = jnp.float32

    near = [device(x, y + k, z, core) for k in (1, 2, 3)] + [device(x, y, z, core + 1)]
    near += [device(x, y, z + k, core) for k in (1, 2, 3)] + [device(x + k, y, z, core) for k in (1, 2, 3)]
    barrier = pltpu.get_barrier_semaphore()
    for target in near:
        pl.semaphore_signal(barrier, inc=1, device_id=target, device_id_type=MESH)

    loads = [
        pltpu.make_async_copy(
            src_ref.at[pl.ds(h * HALF, HALF)], src.at[h, y, core, pl.ds(0, HALF)], in_sem.at[h]
        )
        for h in range(2)
    ]
    loads += [
        pltpu.make_async_copy(
            tgt_ref.at[pl.ds(h * 256, 256)], tgt.at[2 * z_lo + h, pl.ds(0, 256)], in_sem.at[2 + h]
        )
        for h in range(2)
    ]
    loads += [
        pltpu.make_async_copy(src_labels_ref, src_labels, in_sem.at[4]),
        pltpu.make_async_copy(tgt_labels_ref, tgt_labels, in_sem.at[5]),
        pltpu.make_async_copy(table_ref, table, in_sem.at[6]),
    ]
    for load in loads:
        load.start()
    loads[4].wait()
    for h in range(2):
        loads[h].wait()
        src[h, y, core, pl.ds(HALF, AUX), 0:HALF] = aux_rows(
            src[h, y, core, pl.ds(0, HALF)], src_labels[:, h * HALF : (h + 1) * HALF]
        )
    loads[5].wait()
    for h in range(2):
        loads[2 + h].wait()
        tgt[2 * z_lo + h, pl.ds(256, AUX)] = aux_rows(
            tgt[2 * z_lo + h, pl.ds(0, 256)], tgt_labels[:, h * 256 : (h + 1) * 256]
        )

    pl.semaphore_wait(barrier, len(near))

    def send(ref, k, target):
        copy = pltpu.make_async_remote_copy(
            src_ref=ref, dst_ref=ref, send_sem=gather_send.at[k], recv_sem=gather_recv.at[k],
            device_id=target, device_id_type=MESH,
        )
        copy.start()
        return copy

    def arrived(ref, k):
        pltpu.make_async_copy(ref, ref, gather_recv.at[k]).wait()

    started = []
    for h in range(2):
        own = src.at[h, y, core]
        started += [send(own, 7 * h + k, device(x, y + k, z, core)) for k in (2, 1, 3)]
        started.append(send(own, 7 * h, device(x, y, z, core + 1)))
        if h == 0:
            started += [
                send(tgt.at[2 * z_lo + q], 14 + q, device(x, y, z + 1 + 2 * q, core)) for q in range(2)
            ]
    for k in (1, 2, 3):
        pl.semaphore_signal(plane_sem, inc=1, device_id=device(x + k, y, z, core), device_id_type=MESH)

    def cols_of(piece):
        h, chunk, c = piece
        return pl.ds(pl.multiple_of(((h * CHUNKS + chunk) * 2 + c) * HALF, HALF), HALF)

    def prepare_source(pieces, slot):
        aux = [src[h, chunk, c, pl.ds(HALF, AUX), 0:HALF].astype(f32) for h, chunk, c in pieces]
        aux = jnp.concatenate(aux, axis=1)
        row = lax.broadcasted_iota(jnp.int32, (LANES, 256), 0)
        side = jnp.where(row.astype(f32) == aux[0:1], 1.0, 0.0)
        side = jnp.where((row >= 67) & (row < 70), 1.0, side)
        for k in range(3):
            side = jnp.where(row == LABELS + k, aux[1 + k : 2 + k], side)
        src_side[slot] = side.astype(jnp.bfloat16)

    def prepare_target(quarter):
        aux = tgt[quarter, pl.ds(256, AUX)].astype(f32)
        row = lax.broadcasted_iota(jnp.int32, (LABELS, 256), 0)
        onehot = jnp.where(row.astype(f32) == aux[0:1], 1.0, 0.0).astype(jnp.bfloat16)
        costs = jnp.dot(table[...], onehot, preferred_element_type=f32) * -128.0
        rest = jnp.where(row < 3, 1.0, 0.0)
        for k in range(3):
            rest = jnp.where(row == 3 + k, aux[1 + k : 2 + k], rest)
        tgt_side[quarter] = jnp.concatenate([costs, rest], axis=0).T.astype(jnp.bfloat16)

    def costs(quarter, pieces, slot):
        rows = jnp.concatenate([src[h, chunk, c, pl.ds(0, HALF)] for h, chunk, c in pieces], axis=0)
        dot = lax.dot_general(tgt[quarter, pl.ds(0, 256)], rows, NT, preferred_element_type=f32)
        dot += jnp.dot(tgt_side[quarter], src_side[slot], preferred_element_type=f32)
        dot = dot * (COST_TO_BITS / 128.0)
        top = jnp.max(dot.reshape(32, 8, 256), axis=0)
        for i, piece in enumerate(pieces):
            at = slice(i * HALF, (i + 1) * HALF)
            block[pl.ds(pl.multiple_of(quarter * 256, 256), 256), cols_of(piece)] = dot[:, at]
            peak[quarter, :, cols_of(piece)] = top[:, at]

    def first_rows(pieces):
        tops = [jnp.max(jnp.max(peak[:, :, cols_of(p)], axis=0), axis=0, keepdims=True) for p in pieces]

        def add(step, totals):
            rows = pl.ds(pl.multiple_of(step * 256, 256), 256)
            values = [jnp.exp2(block[rows, cols_of(p)] - top) for p, top in zip(pieces, tops)]
            return tuple(t + jnp.sum(v.reshape(8, 32, HALF), axis=0) for t, v in zip(totals, values))

        totals = lax.fori_loop(0, ROWS // 256, add, (jnp.zeros((32, HALF), f32),) * 2)
        for (h, chunk, c), top, total in zip(pieces, tops, totals):
            s_msg[0, h, 0, c, pl.ds(chunk, 1)] = top + jnp.log2(jnp.sum(total, axis=0, keepdims=True))

    def whole(pieces):
        slot = pieces[0][0]
        prepare_source(pieces, slot)
        for quarter in range(QUARTERS):
            costs(quarter, pieces, slot)
        first_rows(pieces)

    def chunk_at(k):
        return lax.rem(y + 4 - k, 4)

    def take(h, k):
        ref = src.at[h, chunk_at(k), core]
        arrived(ref, 7 * h + k)
        started.append(send(ref, 7 * h + 3 + k, device(x, y, z, core + 1)))

    def exchange_s(turn, h):
        for dy, dc in s_peers:
            pltpu.make_async_remote_copy(
                src_ref=s_msg.at[turn, h, 0], dst_ref=s_msg.at[turn, h, dy * 2 + dc],
                send_sem=s_send.at[turn, h], recv_sem=s_recv.at[turn, h],
                device_id=device(x, y + dy, z, core + dc), device_id_type=MESH,
            ).start()

    def exchanged_s(turn, h):
        others = s_msg.at[turn, h, pl.ds(1, 7)]
        pltpu.make_async_copy(others, others, s_recv.at[turn, h]).wait()

    def send_t(turn):
        for dx, dz in t_peers:
            pltpu.make_async_remote_copy(
                src_ref=t_msg.at[turn, 0], dst_ref=t_msg.at[turn, dx * 4 + dz],
                send_sem=t_send.at[turn], recv_sem=t_recv.at[turn],
                device_id=device(x + dx, y, z + dz, core), device_id_type=MESH,
            ).start()

    def received_t(turn):
        others = t_msg.at[turn, pl.ds(1, 15)]
        pltpu.make_async_copy(others, others, t_recv.at[turn]).wait()

    away = 2 * (1 - z_lo)
    own = [[(h, y, c) for c in range(2)] for h in range(2)]
    loads[6].wait()
    for quarter in range(2):
        prepare_target(2 * z_lo + quarter)
    for h in range(2):
        arrived(src.at[h, y, 1 - core], 7 * h)
        prepare_source(own[h], h)
        for quarter in range(2):
            costs(2 * z_lo + quarter, own[h], h)
    for quarter in range(2):
        arrived(tgt.at[away + quarter], 14 + quarter)
        prepare_target(away + quarter)
        for h in range(2):
            costs(away + quarter, own[h], h)
    for h in range(2):
        first_rows(own[h])
    for h in range(2):
        if h == 0:
            for k in (1, 3, 2):
                take(h, k)
        whole([(h, chunk_at(1), core), (h, chunk_at(3), core)])
        other = 1 - core
        arrived(src.at[h, chunk_at(1), other], 7 * h + 4)
        whole([(h, chunk_at(2), core), (h, chunk_at(1), other)])
        arrived(src.at[h, chunk_at(3), other], 7 * h + 6)
        arrived(src.at[h, chunk_at(2), other], 7 * h + 5)
        if h == 0:
            for k in (1, 3, 2):
                take(1, k)
        whole([(h, chunk_at(3), other), (h, chunk_at(2), other)])
        exchange_s(0, h)

    source_count = COLS * 16.0
    target_count = ROWS * 8.0

    def joined(parts):
        top = jnp.max(parts, axis=0)
        return top + jnp.log2(jnp.sum(jnp.exp2(parts - top), axis=0))

    def spread_rows(h, values):
        for i in range(2 * CHUNKS):
            spread[:, tile(h * 2 * CHUNKS + i)] = jnp.broadcast_to(values[i % 2, i // 2 : i // 2 + 1], (8, HALF))

    def tile(l):
        return slice(l * LANES, (l + 1) * LANES)

    def tiles_of(h):
        return range(h * TILES // 2, (h + 1) * TILES // 2)

    def as_columns(values, b):
        return jnp.broadcast_to(values[b : b + 1], (LANES, LANES)).T

    def rows_in(b):
        return [slice(b * LANES + i * 8, b * LANES + i * 8 + 8) for i in range(LANES // 8)]

    def lane_reduced(op, tiles):
        return op(jnp.concatenate(tiles, axis=0).T, axis=0, keepdims=True)

    def first_columns(h):
        across = [spread[:, tile(l)] for l in tiles_of(h)]
        logs = []
        for b in range(8):
            tops = []
            for rows in rows_in(b):
                top = None
                for l, given in zip(tiles_of(h), across):
                    value = block[rows, tile(l)] + given
                    top = value if top is None else jnp.maximum(top, value)
                tops.append(top)
            top = lane_reduced(jnp.max, tops)
            top_dense[h, b : b + 1] = top
            col_max[h, tile(b), :] = jnp.broadcast_to(top, (LANES, LANES)).T
        for b in range(8):
            totals = []
            for rows in rows_in(b):
                top_column, total = col_max[h, rows, :], None
                for l, given in zip(tiles_of(h), across):
                    value = jnp.exp2(block[rows, tile(l)] + (given - top_column))
                    plan[rows, tile(l)] = value
                    total = value if total is None else total + value
                totals.append(total)
            logs.append(jnp.log2(lane_reduced(jnp.sum, totals)))
        return top_dense[h] + jnp.concatenate(logs, axis=0)

    logs = []
    for h in range(2):
        exchanged_s(0, h)
        f_now = math.log2(target_count) - joined(s_msg[0, h])
        f_first[h] = f_now
        spread_rows(h, f_now)
        logs.append(first_columns(h))
    top = jnp.maximum(logs[0], logs[1])
    t_msg[0, 0] = top + jnp.log2(jnp.exp2(logs[0] - top) + jnp.exp2(logs[1] - top))
    pl.semaphore_wait(plane_sem, 3)
    send_t(0)

    def rescale(step, _):
        for s in range(8):
            rows = pl.ds(pl.multiple_of(step * 64 + s * 8, 8), 8)
            both = jnp.maximum(col_max[0, rows, :], col_max[1, rows, :])
            for h in range(2):
                down = jnp.exp2(col_max[h, rows, :] - both)
                for l in tiles_of(h):
                    block[rows, tile(l)] = plan[rows, tile(l)] * down
        return 0

    lax.fori_loop(0, ROWS // 64, rescale, 0)
    top = jnp.maximum(top_dense[0], top_dense[1])
    received_t(0)
    g_now = math.log2(source_count) - joined(t_msg[0])
    g_first[...] = g_now
    scale = jnp.exp2(top + g_now)
    def row_sums(turn, h, factors):
        totals = [None for _ in tiles_of(h)]
        for b in range(8):
            if h == 0:
                weight[tile(b), :] = as_columns(factors, b)
            for rows in rows_in(b):
                w = weight[rows, :]
                values = [block[rows, tile(l)] * w for l in tiles_of(h)]
                totals = [v if t is None else t + v for t, v in zip(totals, values)]
        for i, total in enumerate(totals):
            s_msg[turn, h, 0, i % 2, i // 2 : i // 2 + 1] = jnp.sum(total, axis=0, keepdims=True)

    def column_sums(h, b, across):
        totals = []
        for rows in rows_in(b):
            total = None if h == 0 else partial[rows, :]
            for l, given in zip(tiles_of(h), across):
                value = block[rows, tile(l)] * given
                total = value if total is None else total + value
            if h == 0:
                partial[rows, :] = total
            totals.append(total)
        return totals

    factors = scale
    for turn in (1, 2):
        for h in range(2):
            row_sums(turn, h, factors)
            exchange_s(turn, h)
        sums = []
        for h in range(2):
            exchanged_s(turn, h)
            u_now = target_count / jnp.sum(s_msg[turn, h], axis=0)
            spread_rows(h, u_now)
            across = [spread[:, tile(l)] for l in tiles_of(h)]
            for b in range(8):
                totals = column_sums(h, b, across)
                if h == 1:
                    sums.append(lane_reduced(jnp.sum, totals))
            if turn == 2:
                f_first[h] = (f_first[h] + jnp.log2(u_now)) * (1.0 / COST_TO_BITS)
        t_msg[turn, 0] = scale * jnp.concatenate(sums, axis=0)
        send_t(turn)
        received_t(turn)
        v_now = source_count / jnp.sum(t_msg[turn], axis=0)
        factors = scale * v_now

    for h in range(2):
        out[h : h + 1] = f_first[h, core, pl.ds(y, 1)]
    g_first[...] = (g_first[...] + jnp.log2(v_now)) * (1.0 / COST_TO_BITS)
    out[4:8] = g_first[pl.ds(z_lo * 4, 4)]

    for copy in started:
        copy.wait_send()
    for turn in range(3):
        for h in range(2):
            others = s_msg.at[turn, h, pl.ds(1, 7)]
            pltpu.make_async_copy(others, others, s_send.at[turn, h]).wait()
        others = t_msg.at[turn, pl.ds(1, 15)]
        pltpu.make_async_copy(others, others, t_send.at[turn]).wait()


def hand_on(both, f_out, g_out):
    f_out[...] = both[0:2]
    g_out[...] = both[4:8]


def body(source_embed, source_labels, target_embed, target_labels, label_table):
    vmem, hbm = pl.BlockSpec(memory_space=pltpu.VMEM), pl.BlockSpec(memory_space=pltpu.HBM)
    f32, bf16, dma = jnp.float32, jnp.bfloat16, pltpu.SemaphoreType.DMA
    both = pl.pallas_call(
        kernel,
        out_shape=jax.ShapeDtypeStruct((8, LANES), f32),
        in_specs=[hbm] * 5,
        out_specs=vmem,
        scratch_shapes=[
            pltpu.VMEM((1, SRC), jnp.int32),
            pltpu.VMEM((1, TGT), jnp.int32),
            pltpu.VMEM((LABELS, LABELS), bf16),
            pltpu.VMEM((2, CHUNKS, 2, HALF + AUX, EMB), bf16),
            pltpu.VMEM((QUARTERS, 256 + AUX, EMB), bf16),
            pltpu.VMEM((2, LANES, 256), bf16),
            pltpu.VMEM((QUARTERS, 256, LANES), bf16),
            pltpu.VMEM((ROWS, COLS), f32),
            pltpu.VMEM((ROWS, COLS), f32),
            pltpu.VMEM((QUARTERS, 8, COLS), f32),
            pltpu.VMEM((2, ROWS, LANES), f32),
            pltpu.VMEM((ROWS, LANES), f32),
            pltpu.VMEM((ROWS, LANES), f32),
            pltpu.VMEM((8, COLS), f32),
            pltpu.VMEM((3, 2, 8, 2, CHUNKS, LANES), f32),
            pltpu.VMEM((3, 16, 8, LANES), f32),
            pltpu.VMEM((2, 2, CHUNKS, LANES), f32),
            pltpu.VMEM((2, 8, LANES), f32),
            pltpu.VMEM((8, LANES), f32),
            dma((7,)),
            dma((16,)),
            dma((16,)),
            dma((3, 2)),
            dma((3, 2)),
            dma((3,)),
            dma((3,)),
            pltpu.SemaphoreType.REGULAR,
        ],
        compiler_params=pltpu.CompilerParams(collective_id=0, has_side_effects=True, vmem_limit_bytes=60 << 20),
    )(
        source_embed,
        source_labels.reshape(1, SRC),
        target_embed,
        target_labels.reshape(1, TGT),
        label_table,
    )
    f, g = pl.pallas_call(
        hand_on,
        out_shape=(jax.ShapeDtypeStruct((2, HALF), f32), jax.ShapeDtypeStruct((4, LANES), f32)),
        in_specs=[vmem],
        out_specs=(vmem, vmem),
    )(both)
    return f.reshape(SRC), g.reshape(TGT)


def solution(mesh):
    placed = (P(("dp", "stream"), None), P(("dp", "stream")), P("stream", None), P("stream"), P())
    return jax.shard_map(
        body,
        mesh=mesh,
        in_specs=placed,
        out_specs=(P(("dp", "stream")), P("stream")),
        check_vma=False,
    )
```
